256 devices in a mesh: tiles: 32 (over z, y), fft: 8 (over x, core).
Axes of the slice: x: 4, y: 4, z: 8, core: 2. Of those that a mesh axis runs over, the one named last changes fastest.
Arguments:
- cotangent: bfloat16 [65536, 4096], P(('tiles', 'fft')), may hold values from -6 to 6
- base_grad: bfloat16 [65536, 4096], P(('tiles', 'fft')), may hold values from -6 to 6
- tile_place: int32 [65536], P(('tiles', 'fft')), may hold values from 0 to 1048575, as said below
- tile_count: int32 [256], P(('tiles', 'fft')), may hold values from 64 to 256, as said below
- psf_spectrum: float32 [2, 1536, 2048], P(None, None, 'fft'), may hold values from -2.4 to 2.4
Outputs:
- mask_grad: bfloat16 [65536, 4096], P(('tiles', 'fft'))
The draws below stay inside these ranges and needn't reach their ends.
Inputs may be any that keep to these rules, and one draw needn't show every extreme that they name: `tile_place`: slots form groups of 256; the live slots of group q hold distinct tiles whose tile row lies in band q mod 8 (tile rows (q mod 8) * 16 up to the next band); at most 8 live tiles of one group lie in one block of 1024 columns, and some group reaches that; no tile appears in two slots; slots past the count hold 0. `tile_count`: some group of every band is full.
All inputs are finite; a program needn't handle non-finite values.
Results may differ from the reference program's by a relative error of at most 0.001.
Values sent between devices are 32-bit elements; how exact they have to be, the bound alone decides.
No kernel may reach another device: no remote copies, remote signals or barrier semaphores. Data moves between devices by JAX's collectives and lax.ppermute only.
A program may use at most 192 MiB of HBM per device.

```python
import jax
import jax.numpy as jnp
from jax import lax

ROWS_DEV = 64
BLOCK = 1024
REACH = 512
SUB = 16
TCELL = 4
BUCKET = 8
SLOTS_DEV = 256
SLOTS = 65536
FINE = 64
ROWS = 512
NCOLS = 32768
L0 = 1536
L1 = 2048
N_TILES = 32
N_FFT = 8


def layout(key):
    devices_all = N_TILES * N_FFT
    key_list = jax.random.split(key, 5)
    halving = jax.random.randint(key_list[0], (devices_all,), 0, 3)
    counts = jnp.right_shift(jnp.full((devices_all,), SLOTS_DEV, jnp.int32), halving.astype(jnp.int32))
    dev_numbers = jnp.arange(devices_all, dtype=jnp.int32)
    band_of = dev_numbers % N_FFT
    holder_of = dev_numbers // N_FFT
    fullest = jax.random.randint(key_list[1], (N_FFT,), 0, N_TILES)
    counts = jnp.where(holder_of == fullest[band_of], SLOTS_DEV, counts).astype(jnp.int32)
    offsets = jax.random.randint(key_list[2], (devices_all,), 0, N_TILES)
    orders = jax.vmap(lambda sub_key: jax.random.permutation(sub_key, SLOTS_DEV))(jax.random.split(key_list[3], devices_all))
    slot_numbers = jnp.arange(SLOTS_DEV, dtype=jnp.int32)
    active = slot_numbers[None, :] < counts[:, None]
    earlier = (orders[:, None, :] < orders[:, :, None]) & active[:, None, :]
    slot_ranks = jnp.sum(earlier.astype(jnp.int32), axis=2)
    blocks_of = (offsets[:, None] + slot_ranks) % N_TILES
    depth_index = slot_ranks // N_TILES
    spots_per = ROWS_DEV // TCELL * (BLOCK // TCELL)
    spot_orders = jax.vmap(lambda sub_key: jax.random.permutation(sub_key, spots_per))(jax.random.split(key_list[4], N_FFT * N_TILES))
    spot_orders = spot_orders.reshape(N_FFT, N_TILES, spots_per)
    choose = jnp.minimum(holder_of[:, None] * BUCKET + depth_index, spots_per - 1)
    spot_values = spot_orders[band_of[:, None], blocks_of, choose]
    tile_cols = BLOCK // TCELL
    row_tile = band_of[:, None] * (ROWS_DEV // TCELL) + spot_values // tile_cols
    col_tile = blocks_of * tile_cols + spot_values % tile_cols
    places = jnp.where(active, row_tile * (N_TILES * tile_cols) + col_tile, 0)
    return (places.reshape(-1).astype(jnp.int32), counts)


def draw_tile_place(key, part):
    return layout(key)[0]


def draw_tile_count(key, part):
    return layout(key)[1]


def steps_of(stream_key, dims, shards, low, top_value):
    gain, own = 1.0, jax.random.fold_in(stream_key, 6)
    for position, blocks in shards:
        steps = jnp.exp(jax.random.uniform(jax.random.fold_in(own, position), (blocks,), jnp.float32, low / len(shards), top_value / len(shards)))
        gain = gain * jnp.repeat(steps, dims[position] // blocks).reshape([-1 if axis == position else 1 for axis in range(len(dims))])
    return gain


def scatter_about(rng, shape, scale, most, cuts=(), kind=jnp.bfloat16):
    values = scale * jax.random.normal(rng, shape, jnp.float32)
    if cuts:
        values = values * steps_of(rng, shape, cuts, -0.22, 0.18)
    return jnp.clip(values, -most, most).astype(kind)


def setup_inputs(seed: int = 0) -> dict:
    seeds = jax.random.split(jax.random.key(seed), 6)
    return {
        "cotangent": scatter_about(seeds[0], (SLOTS, FINE * FINE), 1.0, 6.0, ((0, 256),)),
        "base_grad": scatter_about(seeds[1], (SLOTS, FINE * FINE), 1.0, 6.0, ((0, 256),)),
        "tile_place": draw_tile_place(jax.random.fold_in(seeds[5], 71), 0),
        "tile_count": draw_tile_count(jax.random.fold_in(seeds[5], 71), 0),
        "psf_spectrum": scatter_about(seeds[4], (2, L0, L1), 0.3, 2.4, ((2, 8),), jnp.float32),
    }


def reference(cotangent, base_grad, tile_place, tile_count, psf_spectrum):
    slot_total = tile_place.shape[0]
    slot_numbers = jnp.arange(slot_total, dtype=jnp.int32)
    active = (slot_numbers % SLOTS_DEV) < tile_count[slot_numbers // SLOTS_DEV]
    pooled = jnp.sum(cotangent.astype(jnp.float32).reshape(slot_total, TCELL, SUB, TCELL, SUB), axis=(2, 4))
    pooled = jnp.where(active[:, None, None], pooled, 0.0)
    tile_rows = ROWS // TCELL
    tile_cols = NCOLS // TCELL
    places = jnp.where(active, tile_place, tile_rows * tile_cols).astype(jnp.int32)
    patches = jnp.zeros((tile_rows * tile_cols + 1, TCELL, TCELL), jnp.float32).at[places].add(pooled)[:-1]
    density_grad = patches.reshape(tile_rows, tile_cols, TCELL, TCELL).transpose(0, 2, 1, 3).reshape(ROWS, NCOLS)
    padded = jnp.pad(density_grad, ((REACH, REACH), (REACH, REACH)))
    transfer = psf_spectrum[0] + 1j * psf_spectrum[1]

    def one_block(block_index):
        window = lax.dynamic_slice_in_dim(padded, block_index * BLOCK, L1, 1)
        spectrum = jnp.fft.fft2(window)
        restored = jnp.real(jnp.fft.ifft2(spectrum * transfer))
        return restored[REACH:REACH + ROWS, REACH:REACH + BLOCK].astype(jnp.float32)

    blocks = lax.map(one_block, jnp.arange(N_TILES, dtype=jnp.int32))
    sensitivity = blocks.transpose(1, 0, 2).reshape(ROWS, NCOLS)
    sens_patches = sensitivity.reshape(tile_rows, TCELL, tile_cols, TCELL).transpose(0, 2, 1, 3)
    sens_patches = sens_patches.reshape(tile_rows * tile_cols, TCELL, TCELL)
    picked = jnp.take(sens_patches, jnp.where(active, tile_place, 0).astype(jnp.int32), axis=0)
    picked = jnp.where(active[:, None, None], picked, 0.0)
    upsampled = jnp.broadcast_to(picked[:, :, None, :, None], (slot_total, TCELL, SUB, TCELL, SUB))
    upsampled = upsampled.reshape(slot_total, FINE * FINE)
    return (base_grad.astype(jnp.float32) + upsampled).astype(jnp.bfloat16)
```

```python
import functools
import math

import jax
import jax.numpy as jnp
import ml_dtypes
import numpy as np
from jax import lax
from jax.experimental import pallas as pl
from jax.experimental.pallas import tpu as pltpu
from jax.sharding import PartitionSpec as P

BANDS = 8
BLOCKS = 32
BUCKET = 8
SLOTS = 256
SUB = 16
TCELL = 4
CELLS = 16
TILE_ROWS = 16
TILE_COLS = 256
ROWS = 512
L0 = 1536
L1 = 2048
STRIP = 256
HALF = 128
PART0 = L0 // 4
WIDE = 512
BF = jnp.bfloat16
F32 = jnp.float32
VMEM_LIMIT = 52 * 1024 * 1024


def split_np(table):
    high = table.astype(ml_dtypes.bfloat16)
    low = (table - high.astype(np.float64)).astype(ml_dtypes.bfloat16)
    return high, low


@functools.lru_cache(maxsize=None)
def tables():
    k = np.arange(L1)
    u = np.arange(L1 // 2).reshape(256, 4).T.reshape(-1)
    angle = (np.outer(2 * u + 1, k) % (2 * L1)) * (math.pi / L1)
    cos, sin = np.cos(angle), np.sin(angle)

    def strips(table):
        return table.reshape(table.shape[0], BANDS, STRIP).transpose(1, 0, 2)

    ch, cl = split_np(strips(cos))
    sh, sl = split_np(strips(-sin))
    fwd = np.stack([ch, cl, sh, sl], axis=1)
    near = (u < 2 * STRIP)
    scale = 1.0 / (L0 * L1)
    ch, cl = split_np(strips(cos[near]).transpose(0, 2, 1) * scale)
    sh, sl = split_np(strips(sin[near]).transpose(0, 2, 1) * scale)
    back = np.stack([ch, cl, sh, sl], axis=1)
    k0 = np.arange(PART0)
    rows = []
    for i in range(4):
        angle = (np.outer(k0, 4 * np.arange(128) + i) % L0) * (2 * math.pi / L0)
        c, s = np.cos(angle), np.sin(angle)
        rows.append(np.block([[c, s], [-s, c]]))
    rows = np.stack(rows)
    rfwd = np.stack(split_np(rows))
    rback = np.stack(split_np(rows.transpose(0, 2, 1)))
    return fwd, back, rfwd, rback


def split(x):
    high = x.astype(BF)
    low = (x - high.astype(F32)).astype(BF)
    return high, low


def split3(x):
    high = x.astype(BF)
    rest = x - high.astype(F32)
    mid = rest.astype(BF)
    low = (rest - mid.astype(F32)).astype(BF)
    return high, mid, low


def dot(a, b):
    return jnp.dot(a, b, preferred_element_type=F32)


def dot_nt(a, b):
    return lax.dot_general(a, b, (((1,), (1,)), ((), ())), preferred_element_type=F32)


def iota(shape, dim):
    return lax.broadcasted_iota(jnp.int32, shape, dim)


def pool_kernel(count_ref, place_ref, cot_hbm, msg_ref, meta_ref, cot, sems):
    copies = [
        pltpu.make_async_copy(
            cot_hbm.at[:, pl.ds(i * 1024, 1024)], cot.at[:, pl.ds(i * 1024, 1024)], sems.at[i]
        )
        for i in range(4)
    ]
    for copy in copies:
        copy.start()
    count = count_ref[0]
    place_row = place_ref[...]
    square = (SLOTS, SLOTS)
    down, across = iota(square, 0), iota(square, 1)

    def fields(place, live):
        column = place & (BLOCKS * TILE_COLS - 1)
        row = (place >> 13) & (TILE_ROWS - 1)
        target = jnp.where(live, column >> 8, -8)
        return row, target, column & (TILE_COLS - 1)

    live_row = iota((1, SLOTS), 1) < count
    _, target_row, tc_row = fields(place_row, live_row)
    place_col = jnp.sum(
        jnp.where(down == across, place_row.astype(F32), 0.0), axis=1, keepdims=True
    ).astype(jnp.int32)
    live_col = iota((SLOTS, 1), 0) < count
    tr_col, target_col, tc_col = fields(place_col, live_col)
    before = (target_row == target_col) & (across < down) & live_row
    rank_col = jnp.sum(jnp.where(before, 1.0, 0.0), axis=1, keepdims=True).astype(jnp.int32)
    right_col = tc_col >= HALF
    lane = iota((SLOTS, 128), 1)
    meta_ref[...] = jnp.where(
        lane == 0, target_col, jnp.where(lane == 1, rank_col, right_col.astype(jnp.int32))
    )
    b = iota((BLOCKS, SLOTS), 0)
    right_row = tc_row >= HALF
    hot_own = target_row == b
    hot_left = (target_row == b - 1) & right_row & live_row
    hot_right = (target_row == b + 1) & (~right_row) & live_row
    hot = jnp.concatenate(
        [jnp.where(h, 1.0, 0.0) for h in (hot_own, hot_left, hot_right)], axis=0
    ).astype(BF)
    code_own = 1 + tr_col * 256 + jnp.where(right_col, tc_col - HALF, 255 - tc_col)
    code_halo = 1 + tr_col * 256 + jnp.where(right_col, 255 - tc_col, tc_col)
    mark_own = jnp.where(lane == rank_col, code_own, 0).astype(F32)
    mark_halo = jnp.where((lane & 7) == rank_col, code_halo, 0).astype(F32)
    prow, plane = iota((256, 256), 0), iota((256, 256), 1)
    want_j = (plane >> 2) & 3
    want_j = jnp.where(plane >= 128, 3 - want_j, want_j)
    match_j = ((prow >> 4) & 3) == want_j
    total = jnp.zeros((SLOTS, 256), F32)
    for i in range(4):
        weights = jnp.where(match_j & ((plane & 3) == i), 1.0, 0.0).astype(BF)
        copies[i].wait()
        for c in range(4):
            total = total + dot(cot[:, i * 1024 + c * 256 : i * 1024 + (c + 1) * 256], weights)
    plain, flipped = total[:, :128], total[:, 128:]
    here = (lane >> 4) == rank_col
    own = jnp.where(here, jnp.where(right_col, plain, flipped), 0.0)
    halo = jnp.where(here, jnp.where(right_col, flipped, plain), 0.0)
    loads = jnp.concatenate([own, halo, mark_own, mark_halo], axis=1)
    out = jnp.zeros((3 * BLOCKS, 512), F32)
    for piece in split3(loads):
        out = out + dot(hot, piece)
    lane32 = iota((BLOCKS, 128), 1)
    marks = jnp.where(
        lane32 < 8,
        out[0:32, 256:384],
        jnp.where(lane32 < 16, out[32:64, 384:512], jnp.where(lane32 < 24, out[64:96, 384:512], 0.0)),
    )
    message = jnp.concatenate(
        [out[0:32, 0:128], out[32:64, 128:256], out[64:96, 128:256], marks], axis=1
    )
    for f in range(BANDS):
        msg_ref[f * BLOCKS : (f + 1) * BLOCKS, :] = message


def pool(cotangent, tile_place, tile_count):
    return pl.pallas_call(
        pool_kernel,
        out_shape=(
            jax.ShapeDtypeStruct((BANDS * BLOCKS, WIDE), F32),
            jax.ShapeDtypeStruct((SLOTS, 128), jnp.int32),
        ),
        in_specs=[
            pl.BlockSpec(memory_space=pltpu.SMEM),
            pl.BlockSpec(memory_space=pltpu.VMEM),
            pl.BlockSpec(memory_space=pl.ANY),
        ],
        out_specs=(
            pl.BlockSpec(memory_space=pltpu.VMEM),
            pl.BlockSpec(memory_space=pltpu.VMEM),
        ),
        scratch_shapes=[pltpu.VMEM((SLOTS, 4096), BF), pltpu.SemaphoreType.DMA((4,))],
        compiler_params=pltpu.CompilerParams(vmem_limit_bytes=VMEM_LIMIT),
        name="pool",
    )(tile_count, tile_place.reshape(1, SLOTS), cotangent)


def chunk_swap(pieces, lane):
    out = []
    for band in range(4):
        value = None
        for e in range(4):
            moved = pieces[e] if e == band else pltpu.roll(pieces[e], ((e - band) * 32) % 128, 1)
            value = moved if value is None else jnp.where((lane >> 5) == e, moved, value)
        out.append(value)
    return out


def conv_kernel(
    f_ref, recv_ref, fwd_hbm, rfwd_hbm, psf_hbm, rback_hbm, back_hbm, out_ref,
    fwd, rfwd, psf, rback, back, tv, tm, e_s, o_s, y_s, q_s, s_s, tg, sems,
):
    f = f_ref[0, 0]
    copies = [
        pltpu.make_async_copy(fwd_hbm.at[f], fwd, sems.at[0]),
        pltpu.make_async_copy(rfwd_hbm, rfwd, sems.at[1]),
        pltpu.make_async_copy(psf_hbm, psf, sems.at[2]),
        pltpu.make_async_copy(rback_hbm, rback, sems.at[3]),
        pltpu.make_async_copy(back_hbm.at[f], back, sems.at[4]),
    ]
    for copy in copies:
        copy.start()

    turned = jnp.transpose(recv_ref[...])
    lane16 = iota((16, 128), 1)
    lane8 = iota((8, 128), 1)
    for nbr in range(3):
        for eh in range(2):
            for bh in range(2):
                group = [
                    turned[nbr * 128 + (eh * 4 + e) * 16 : nbr * 128 + (eh * 4 + e + 1) * 16,
                           bh * 128 : (bh + 1) * 128]
                    for e in range(4)
                ]
                for band, value in enumerate(chunk_swap(group, lane16)):
                    tv[bh * 4 + band, nbr, :, eh * 128 : (eh + 1) * 128] = value
                marks = turned[384 + nbr * 8 : 384 + nbr * 8 + 8, bh * 128 : (bh + 1) * 128]
                group = [
                    jnp.broadcast_to(marks[eh * 4 + e : eh * 4 + e + 1, :], (8, 128))
                    for e in range(4)
                ]
                for band, value in enumerate(chunk_swap(group, lane8)):
                    tm[bh * 4 + band, nbr, :, eh * 128 : (eh + 1) * 128] = (
                        value.astype(jnp.int32) - 1
                    )

    row16 = iota((16, 256), 0)

    def hot_of(code, rows):
        spot = jnp.broadcast_to(code[0:1, :] & 255, (rows, 256))
        return jnp.where(iota((rows, 256), 0) == spot, 1.0, 0.0).astype(BF)

    def scatter(band, carry):
        base = pl.multiple_of(band * 16, 16)
        outs = []
        for nbr in range(3):
            code = tm[band, nbr]
            mask = row16 == jnp.broadcast_to(code[0:1, :] >> 8, (16, 256))
            values = tv[band, nbr]
            high = values.astype(BF).astype(F32)
            low = values - high
            parts = []
            for piece in (high, low):
                for c in range(CELLS):
                    parts.append(
                        jnp.where(mask, jnp.broadcast_to(piece[c : c + 1, :], (16, 256)), 0.0).astype(BF)
                    )
            left = jnp.concatenate(parts, axis=0)
            both = dot_nt(left, hot_of(code, 256 if nbr == 0 else 128))
            outs.append(both[:256] + both[256:])
        near_r, near_l = outs[0][:, :128], outs[0][:, 128:]
        far_l, far_r = outs[1], outs[2]
        for ref, near, far in ((e_s, near_r + near_l, far_r + far_l), (o_s, near_r - near_l, far_r - far_l)):
            for part, value in enumerate((near, far)):
                for level, piece in enumerate(split(value)):
                    for j in range(4):
                        for i in range(4):
                            ref[level, pl.ds(i * 128 + base, 16),
                                j * 256 + part * 128 : j * 256 + (part + 1) * 128] = (
                                piece[(j * 4 + i) * 16 : (j * 4 + i + 1) * 16, :]
                            )
        return carry

    lax.fori_loop(0, BANDS, scatter, 0)

    copies[0].wait()
    for i in range(4):
        rows = slice(i * 128, (i + 1) * 128)
        for part, ref in enumerate((e_s, o_s)):
            high, low = ref[0, rows, :], ref[1, rows, :]
            table_high, table_low = fwd[2 * part], fwd[2 * part + 1]
            y = dot(high, table_high) + (dot(high, table_low) + dot(low, table_high))
            y_high, y_low = split(y)
            y_s[0, i, part * 128 : (part + 1) * 128, :] = y_high
            y_s[1, i, part * 128 : (part + 1) * 128, :] = y_low

    copies[1].wait()
    copies[2].wait()
    step = 64

    def middle(chunk, carry):
        start = pl.multiple_of(chunk * step, step)

        def row_part(i, part):
            rows = pl.ds(part * PART0 + start, step)
            high, low = rfwd[0, i, rows, :], rfwd[1, i, rows, :]
            return dot(high, y_s[0, i]) + (dot(high, y_s[1, i]) + dot(low, y_s[0, i]))

        g = [(row_part(i, 0), row_part(i, 1)) for i in range(4)]

        def four(v, sign):
            (ar, ai), (br, bi), (cr, ci), (dr, di) = v
            pr, pi_, mr, mi = ar + cr, ai + ci, ar - cr, ai - ci
            qr, qi, nr, ni = br + dr, bi + di, br - dr, bi - di
            tr_, ti = -sign * ni, sign * nr
            return [(pr + qr, pi_ + qi), (mr + tr_, mi + ti), (pr - qr, pi_ - qi), (mr - tr_, mi - ti)]

        x = four(g, -1.0)
        prod = []
        for m in range(4):
            hr = psf[0, pl.ds(m * PART0 + start, step), :]
            hi = psf[1, pl.ds(m * PART0 + start, step), :]
            xr, xi = x[m]
            prod.append((xr * hr - xi * hi, xr * hi + xi * hr))
        for i, pair in enumerate(four(prod, 1.0)):
            for part in range(2):
                q_high, q_low = split(pair[part])
                rows = pl.ds(part * PART0 + start, step)
                q_s[0, i, rows, :] = q_high
                q_s[1, i, rows, :] = q_low
        return carry

    lax.fori_loop(0, PART0 // step, middle, 0)

    copies[3].wait()
    copies[4].wait()
    for i in range(4):
        high, low = rback[0, i], rback[1, i]
        z = dot(high, q_s[0, i]) + (dot(high, q_s[1, i]) + dot(low, q_s[0, i]))
        z_high, z_low = split(z)
        sums = []
        for part in range(2):
            rows = slice(part * 128, (part + 1) * 128)
            sums.append(
                dot(z_high[rows], back[2 * part])
                + (dot(z_high[rows], back[2 * part + 1]) + dot(z_low[rows], back[2 * part]))
            )
        for side, value in enumerate((sums[0] - sums[1], sums[0] + sums[1])):
            for level, piece in enumerate(split(value)):
                for j in range(4):
                    s_s[level, j, i * 128 : (i + 1) * 128, side * 128 : (side + 1) * 128] = (
                        piece[:, j * 128 : (j + 1) * 128]
                    )

    def gather(band, carry):
        base = pl.multiple_of(band * 16, 16)
        code = tm[band, 0]
        hot = hot_of(code, 256)
        mask = row16 == jnp.broadcast_to(code[0:1, :] >> 8, (16, 256))
        left = jnp.concatenate(
            [s_s[level, j, pl.ds(i * 128 + base, 16), :] for level in range(2) for j in range(4) for i in range(4)],
            axis=0,
        )
        both = dot(left, hot)
        total = both[:256] + both[256:]
        for c in range(CELLS):
            tg[band, c : c + 1, :] = jnp.sum(
                jnp.where(mask, total[c * 16 : (c + 1) * 16, :], 0.0), axis=0, keepdims=True
            )
        return carry

    lax.fori_loop(0, BANDS, gather, 0)
    halves = []
    for eh in range(2):
        quarter = []
        for bh in range(2):
            group = [tg[bh * 4 + band, :, eh * 128 : (eh + 1) * 128] for band in range(4)]
            quarter.append(jnp.concatenate(chunk_swap(group, lane16), axis=0))
        halves.append(jnp.concatenate(quarter, axis=1))
    out_ref[...] = jnp.transpose(jnp.concatenate(halves, axis=0))


def conv(strip, received, psf):
    fwd, back, rfwd, rback = tables()
    any_spec = pl.BlockSpec(memory_space=pl.ANY)
    return pl.pallas_call(
        conv_kernel,
        out_shape=jax.ShapeDtypeStruct((BANDS * BLOCKS, 128), F32),
        in_specs=[
            pl.BlockSpec(memory_space=pltpu.SMEM),
            pl.BlockSpec(memory_space=pltpu.VMEM),
            any_spec, any_spec, any_spec, any_spec, any_spec,
        ],
        out_specs=pl.BlockSpec(memory_space=pltpu.VMEM),
        scratch_shapes=[
            pltpu.VMEM((4, 1024, STRIP), BF),
            pltpu.VMEM((2, 4, 2 * PART0, 256), BF),
            pltpu.VMEM((2, L0, STRIP), F32),
            pltpu.VMEM((2, 4, 256, 2 * PART0), BF),
            pltpu.VMEM((4, STRIP, 512), BF),
            pltpu.VMEM((BANDS, 3, CELLS, 256), F32),
            pltpu.VMEM((BANDS, 3, 8, 256), jnp.int32),
            pltpu.VMEM((2, ROWS, 1024), BF),
            pltpu.VMEM((2, ROWS, 1024), BF),
            pltpu.VMEM((2, 4, 256, STRIP), BF),
            pltpu.VMEM((2, 4, 2 * PART0, STRIP), BF),
            pltpu.VMEM((2, 4, ROWS, 256), BF),
            pltpu.VMEM((BANDS, CELLS, 256), F32),
            pltpu.SemaphoreType.DMA((5,)),
        ],
        compiler_params=pltpu.CompilerParams(vmem_limit_bytes=VMEM_LIMIT),
        name="conv",
    )(strip, received, jnp.asarray(fwd), jnp.asarray(rfwd), psf, jnp.asarray(rback), jnp.asarray(back))


def spread_kernel(meta_ref, back_ref, base_ref, out_ref):
    rows = base_ref.shape[0]
    summed = back_ref[0:BLOCKS, :]
    for f in range(1, BANDS):
        summed = summed + back_ref[f * BLOCKS : (f + 1) * BLOCKS, :]
    meta = meta_ref[...]
    target, rank, right = meta[:, 0:1], meta[:, 1:2], meta[:, 2:3]
    hot = jnp.where(iota((rows, BLOCKS), 1) == target, 1.0, 0.0).astype(BF)
    picked = jnp.zeros((rows, 128), F32)
    for piece in split3(summed):
        picked = picked + dot(hot, piece)
    lane = iota((rows, 128), 1)
    picked = jnp.where((lane >> 4) == rank, picked, 0.0)
    plain = jnp.where(right == 1, picked, 0.0)
    sides = jnp.concatenate([plain, picked - plain], axis=1)
    krow, nlane = iota((256, 512), 0), iota((256, 512), 1)
    have_j = (krow >> 2) & 3
    have_j = jnp.where(krow >= 128, 3 - have_j, have_j)
    match = (have_j == ((nlane >> 4) & 3)) & ((krow & 3) == (nlane >> 7))
    weights = jnp.where(match, 1.0, 0.0).astype(BF)
    up = jnp.zeros((rows, 512), F32)
    for piece in split3(sides):
        up = up + dot(piece, weights)
    for i in range(4):
        value = up[:, i * 128 : (i + 1) * 128]
        for m in range(8):
            spot = slice(i * 1024 + m * 128, i * 1024 + (m + 1) * 128)
            out_ref[:, spot] = (base_ref[:, spot].astype(F32) + value).astype(BF)


def spread(meta, returned, base_grad):
    step = 64
    return pl.pallas_call(
        spread_kernel,
        grid=(SLOTS // step,),
        out_shape=jax.ShapeDtypeStruct((SLOTS, 4096), BF),
        in_specs=[
            pl.BlockSpec((step, 128), lambda g: (g, 0)),
            pl.BlockSpec((BANDS * BLOCKS, 128), lambda g: (0, 0)),
            pl.BlockSpec((step, 4096), lambda g: (g, 0)),
        ],
        out_specs=pl.BlockSpec((step, 4096), lambda g: (g, 0)),
        compiler_params=pltpu.CompilerParams(vmem_limit_bytes=VMEM_LIMIT),
        name="spread",
    )(meta, returned, base_grad)


def exchange(x):
    return lax.all_to_all(x, ("fft", "tiles"), split_axis=0, concat_axis=0, tiled=True)


def local(cotangent, base_grad, tile_place, tile_count, psf_spectrum):
    strip = lax.axis_index("fft").astype(jnp.int32).reshape(1, 1)
    message, meta = pool(cotangent, tile_place, tile_count)
    received = exchange(message)
    partial = conv(strip, received, psf_spectrum)
    returned = exchange(partial)
    return spread(meta, returned, base_grad)


def solution(mesh):
    return jax.shard_map(
        local,
        mesh=mesh,
        in_specs=(
            P(("tiles", "fft"), None),
            P(("tiles", "fft"), None),
            P(("tiles", "fft")),
            P(("tiles", "fft")),
            P(None, None, "fft"),
        ),
        out_specs=P(("tiles", "fft"), None),
        check_vma=False,
    )
```

```python
import functools
import math

import jax
import jax.numpy as jnp
import ml_dtypes
import numpy as np
from jax import lax
from jax.experimental import pallas as pl
from jax.experimental.pallas import tpu as pltpu
from jax.sharding import PartitionSpec as P

BANDS = 8
BLOCKS = 32
BUCKET = 8
SLOTS = 256
SUB = 16
TCELL = 4
CELLS = 16
TILE_ROWS = 16
TILE_COLS = 256
ROWS = 512
L0 = 1536
L1 = 2048
STRIP = 256
HALF = 128
PART0 = L0 // 4
STEP = 128
CHUNKS = PART0 // STEP
PAIRS = BANDS // 2
BF = jnp.bfloat16
F32 = jnp.float32
UNROLL = 4
VMEM_LIMIT = 52 * 1024 * 1024


def split_np(table):
    high = table.astype(ml_dtypes.bfloat16)
    low = (table - high.astype(np.float64)).astype(ml_dtypes.bfloat16)
    return high, low


@functools.lru_cache(maxsize=None)
def tables():
    k = np.arange(L1)
    u = np.arange(L1 // 2).reshape(256, 4).T.reshape(-1)
    angle = (np.outer(2 * u + 1, k) % (2 * L1)) * (math.pi / L1)
    cos, sin = np.cos(angle), np.sin(angle)

    def strips(table):
        return table.reshape(table.shape[0], BANDS, STRIP).transpose(1, 0, 2)

    ch, cl = split_np(strips(cos))
    sh, sl = split_np(strips(-sin))
    fwd = np.stack([ch, cl, sh, sl], axis=1)
    near = (u < 2 * STRIP)
    scale = 1.0 / (L0 * L1)
    ch, cl = split_np(strips(cos[near]).transpose(0, 2, 1) * scale)
    sh, sl = split_np(strips(sin[near]).transpose(0, 2, 1) * scale)
    back = np.stack([ch, cl, sh, sl], axis=1)
    k0 = np.arange(PART0)
    rows = []
    for i in range(4):
        angle = (np.outer(k0, 4 * np.arange(128) + i) % L0) * (2 * math.pi / L0)
        c, s = np.cos(angle), np.sin(angle)
        rows.append(np.block([[c, s], [-s, c]]))
    rows = np.stack(rows)
    both = np.stack(split_np(rows)).reshape(2, 4, 2, CHUNKS, STEP, 256)
    rfwd = both.transpose(1, 3, 0, 2, 4, 5).reshape(4, CHUNKS, 4 * STEP, 256)
    rback = np.concatenate(split_np(rows.transpose(0, 2, 1)), axis=1)
    return fwd, back, rfwd, rback


def split(x):
    high = x.astype(BF)
    low = (x - high.astype(F32)).astype(BF)
    return high, low


def split3(x):
    high = x.astype(BF)
    rest = x - high.astype(F32)
    mid = rest.astype(BF)
    low = (rest - mid.astype(F32)).astype(BF)
    return high, mid, low


def dot(a, b):
    return jnp.dot(a, b, preferred_element_type=F32)


def dot_nt(a, b):
    return lax.dot_general(a, b, (((1,), (1,)), ((), ())), preferred_element_type=F32)


def iota(shape, dim):
    return lax.broadcasted_iota(jnp.int32, shape, dim)


def pool_kernel(count_ref, place_hbm, cot_hbm, msg_ref, meta_ref, place_ref, cot, sems):
    fetch = pltpu.make_async_copy(place_hbm, place_ref, sems.at[4])
    fetch.start()
    copies = [
        pltpu.make_async_copy(
            cot_hbm.at[:, pl.ds(i * 1024, 1024)], cot.at[:, pl.ds(i * 1024, 1024)], sems.at[i]
        )
        for i in range(4)
    ]
    for copy in copies:
        copy.start()
    count = count_ref[0]
    fetch.wait()
    place_row = place_ref[...]
    square = (SLOTS, SLOTS)
    down, across = iota(square, 0), iota(square, 1)

    def fields(place, live):
        column = place & (BLOCKS * TILE_COLS - 1)
        row = (place >> 13) & (TILE_ROWS - 1)
        target = jnp.where(live, column >> 8, -8)
        return row, target, column & (TILE_COLS - 1)

    live_row = iota((1, SLOTS), 1) < count
    _, target_row, tc_row = fields(place_row, live_row)
    place_col = jnp.sum(
        jnp.where(down == across, place_row.astype(F32), 0.0), axis=1, keepdims=True
    ).astype(jnp.int32)
    live_col = iota((SLOTS, 1), 0) < count
    tr_col, target_col, tc_col = fields(place_col, live_col)
    before = (target_row == target_col) & (across < down) & live_row
    rank_col = jnp.sum(jnp.where(before, 1.0, 0.0), axis=1, keepdims=True).astype(jnp.int32)
    right_col = tc_col >= HALF
    lane = iota((SLOTS, 128), 1)
    meta_ref[...] = jnp.where(
        lane == 0, target_col, jnp.where(lane == 1, rank_col, right_col.astype(jnp.int32))
    )
    b = iota((BLOCKS, SLOTS), 0)
    right_row = tc_row >= HALF
    hot_own = target_row == b
    hot_left = (target_row == b - 1) & right_row & live_row
    hot_right = (target_row == b + 1) & (~right_row) & live_row
    hot = jnp.concatenate(
        [jnp.where(h, 1.0, 0.0) for h in (hot_own, hot_left, hot_right)], axis=0
    ).astype(BF)
    code_own = 1 + tr_col * 256 + jnp.where(right_col, tc_col - HALF, 255 - tc_col)
    code_halo = 1 + tr_col * 256 + jnp.where(right_col, 255 - tc_col, tc_col)
    mark_own = jnp.where(lane == rank_col, code_own, 0).astype(F32)
    mark_halo = jnp.where((lane & 7) == rank_col, code_halo, 0).astype(F32)
    prow, plane = iota((256, 256), 0), iota((256, 256), 1)
    want_j = (plane >> 2) & 3
    want_j = jnp.where(plane >= 128, 3 - want_j, want_j)
    match_j = ((prow >> 4) & 3) == want_j
    total = jnp.zeros((SLOTS, 256), F32)
    for i in range(4):
        weights = jnp.where(match_j & ((plane & 3) == i), 1.0, 0.0).astype(BF)
        copies[i].wait()
        for c in range(4):
            total = total + dot(cot[:, i * 1024 + c * 256 : i * 1024 + (c + 1) * 256], weights)
    plain, flipped = total[:, :128], total[:, 128:]
    here = (lane >> 4) == rank_col
    own = jnp.where(here, jnp.where(right_col, plain, flipped), 0.0)
    halo = jnp.where(here, jnp.where(right_col, flipped, plain), 0.0)
    loads = jnp.concatenate([own, halo, mark_own, mark_halo], axis=1)
    out = jnp.zeros((3 * BLOCKS, 512), F32)
    for piece in split3(loads):
        out = out + dot(hot, piece)
    lane32 = iota((BLOCKS, 128), 1)
    marks = jnp.where(
        lane32 < 8,
        out[0:32, 256:384],
        jnp.where(lane32 < 16, out[32:64, 384:512], jnp.where(lane32 < 24, out[64:96, 384:512], 0.0)),
    )
    message = [out[0:32, 0:128], out[32:64, 128:256], out[64:96, 128:256], marks]
    for f in range(PAIRS):
        for a in range(4):
            msg_ref[pl.ds(f * BLOCKS * 4 + a, BLOCKS, stride=4), :] = message[a]


def pool(cotangent, tile_place, tile_count):
    return pl.pallas_call(
        pool_kernel,
        out_shape=(
            jax.ShapeDtypeStruct((PAIRS * BLOCKS * 4, 128), F32),
            jax.ShapeDtypeStruct((SLOTS, 128), jnp.int32),
        ),
        in_specs=[
            pl.BlockSpec(memory_space=pltpu.SMEM),
            pl.BlockSpec(memory_space=pl.ANY),
            pl.BlockSpec(memory_space=pl.ANY),
        ],
        out_specs=(
            pl.BlockSpec(memory_space=pltpu.VMEM),
            pl.BlockSpec(memory_space=pltpu.VMEM),
        ),
        scratch_shapes=[
            pltpu.VMEM((1, SLOTS), jnp.int32),
            pltpu.VMEM((SLOTS, 4096), BF),
            pltpu.SemaphoreType.DMA((5,)),
        ],
        compiler_params=pltpu.CompilerParams(vmem_limit_bytes=VMEM_LIMIT),
        name="pool",
    )(tile_count, tile_place.reshape(1, SLOTS), cotangent)


def chunk_swap(pieces, lane):
    out = []
    for band in range(4):
        value = None
        for e in range(4):
            moved = pieces[e] if e == band else pltpu.roll(pieces[e], ((e - band) * 32) % 128, 1)
            value = moved if value is None else jnp.where((lane >> 5) == e, moved, value)
        out.append(value)
    return out


def conv_kernel(
    f_ref, near_ref, pair_ref, fwd_hbm, rfwd_hbm, psf_hbm, rback_hbm, back_hbm, out_ref,
    fwd, rfwd, psf, rback, back, tv, tm, e_s, o_s, y_s, g_s, q_s, z_s, s_s, tg, sems,
):
    f = f_ref[0, 0]
    copies = [
        pltpu.make_async_copy(fwd_hbm.at[f], fwd, sems.at[0]),
        pltpu.make_async_copy(rfwd_hbm, rfwd, sems.at[1]),
        pltpu.make_async_copy(psf_hbm, psf, sems.at[2]),
        pltpu.make_async_copy(rback_hbm, rback, sems.at[3]),
        pltpu.make_async_copy(back_hbm.at[f], back, sems.at[4]),
    ]
    for copy in copies:
        copy.start()
    core = f & 1

    lane16 = iota((16, 128), 1)
    lane8 = iota((8, 128), 1)
    for half, ref in enumerate((near_ref, pair_ref)):
        turned = [jnp.transpose(ref[pl.ds(a, 128, stride=4), :]) for a in range(4)]
        for nbr in range(3):
            for eh in range(2):
                group = [turned[nbr][(eh * 4 + e) * 16 : (eh * 4 + e + 1) * 16, :] for e in range(4)]
                for x, value in enumerate(chunk_swap(group, lane16)):
                    tv[half * PAIRS + x, nbr, :, eh * 128 : (eh + 1) * 128] = value
                marks = turned[3][nbr * 8 : nbr * 8 + 8, :]
                group = [
                    jnp.broadcast_to(marks[eh * 4 + e : eh * 4 + e + 1, :], (8, 128)) for e in range(4)
                ]
                for x, value in enumerate(chunk_swap(group, lane8)):
                    tm[half * PAIRS + x, nbr, :, eh * 128 : (eh + 1) * 128] = value.astype(jnp.int32) - 1

    row16 = iota((16, 256), 0)

    def band_of(spot):
        return 2 * (spot & (PAIRS - 1)) + (core ^ (spot >> 2))

    def hot_of(code, rows):
        place = jnp.broadcast_to(code[0:1, :] & 255, (rows, 256))
        return jnp.where(iota((rows, 256), 0) == place, 1.0, 0.0).astype(BF)

    def scatter(spot, carry):
        base = pl.multiple_of(band_of(spot) * 16, 16)
        outs = []
        for nbr in range(3):
            code = tm[spot, nbr]
            mask = row16 == jnp.broadcast_to(code[0:1, :] >> 8, (16, 256))
            values = tv[spot, nbr]
            high = values.astype(BF).astype(F32)
            low = values - high
            parts = []
            for piece in (high, low):
                for c in range(CELLS):
                    parts.append(
                        jnp.where(mask, jnp.broadcast_to(piece[c : c + 1, :], (16, 256)), 0.0).astype(BF)
                    )
            left = jnp.concatenate(parts, axis=0)
            both = dot_nt(left, hot_of(code, 256 if nbr == 0 else 128))
            outs.append(both[:256] + both[256:])
        near_r, near_l = outs[0][:, :128], outs[0][:, 128:]
        far_l, far_r = outs[1], outs[2]
        for ref, near, far in ((e_s, near_r + near_l, far_r + far_l), (o_s, near_r - near_l, far_r - far_l)):
            for part, value in enumerate((near, far)):
                for level, piece in enumerate(split(value)):
                    for j in range(4):
                        for i in range(4):
                            ref[pl.ds(level * ROWS + i * 128 + base, 16),
                                j * 256 + part * 128 : j * 256 + (part + 1) * 128] = (
                                piece[(j * 4 + i) * 16 : (j * 4 + i + 1) * 16, :]
                            )
        return carry

    lax.fori_loop(0, BANDS, scatter, 0, unroll=UNROLL)

    copies[0].wait()
    for part, ref in enumerate((e_s, o_s)):
        first = dot(ref[...], fwd[2 * part])
        second = dot(ref[:ROWS, :], fwd[2 * part + 1])
        y = first[:ROWS] + (first[ROWS:] + second)
        for level, piece in enumerate(split(y)):
            for i in range(4):
                y_s[level, i, part * 128 : (part + 1) * 128, :] = piece[i * 128 : (i + 1) * 128]

    copies[1].wait()
    copies[2].wait()

    def four(v, sign):
        (ar, ai), (br, bi), (cr, ci), (dr, di) = v
        pr, pi_, mr, mi = ar + cr, ai + ci, ar - cr, ai - ci
        qr, qi, nr, ni = br + dr, bi + di, br - dr, bi - di
        if sign > 0:
            return [(pr + qr, pi_ + qi), (mr - ni, mi + nr), (pr - qr, pi_ - qi), (mr + ni, mi - nr)]
        return [(pr + qr, pi_ + qi), (mr + ni, mi - nr), (pr - qr, pi_ - qi), (mr - ni, mi + nr)]

    for chunk in range(CHUNKS):
        for i in range(4):
            first = dot(rfwd[i, chunk], y_s[0, i])
            second = dot(rfwd[i, chunk, : 2 * STEP, :], y_s[1, i])
            g_s[chunk, i] = first[: 2 * STEP] + (first[2 * STEP :] + second)
        for r in range(0, STEP, 16):
            for lanes in (slice(0, 128), slice(128, 256)):
                g = [(g_s[chunk, i, r : r + 16, lanes], g_s[chunk, i, STEP + r : STEP + r + 16, lanes])
                     for i in range(4)]
                prod = []
                for m, (xr, xi) in enumerate(four(g, -1)):
                    rows = slice(m * PART0 + chunk * STEP + r, m * PART0 + chunk * STEP + r + 16)
                    hr, hi = psf[0, rows, lanes], psf[1, rows, lanes]
                    prod.append((xr * hr - xi * hi, xr * hi + xi * hr))
                for i, pair in enumerate(four(prod, 1)):
                    for part in range(2):
                        rows = slice(part * PART0 + chunk * STEP + r, part * PART0 + chunk * STEP + r + 16)
                        for level, piece in enumerate(split(pair[part])):
                            q_s[level, i, rows, lanes] = piece

    copies[3].wait()
    for i in range(4):
        first = dot(rback[i], q_s[0, i])
        second = dot(rback[i, :256, :], q_s[1, i])
        z = first[:256] + (first[256:] + second)
        for level, piece in enumerate(split(z)):
            for part in range(2):
                z_s[part, level * ROWS + i * 128 : level * ROWS + (i + 1) * 128, :] = (
                    piece[part * 128 : (part + 1) * 128]
                )
    copies[4].wait()
    for j in range(4):
        lanes = slice(j * 128, (j + 1) * 128)
        sums = []
        for part in range(2):
            first = dot(z_s[part], back[2 * part, :, lanes])
            second = dot(z_s[part, :ROWS, :], back[2 * part + 1, :, lanes])
            sums.append(first[:ROWS] + (first[ROWS:] + second))
        for side, value in enumerate((sums[0] - sums[1], sums[0] + sums[1])):
            for level, piece in enumerate(split(value)):
                s_s[level, j, :, side * 128 : (side + 1) * 128] = piece

    def gather(spot, carry):
        base = pl.multiple_of(band_of(spot) * 16, 16)
        code = tm[spot, 0]
        hot = hot_of(code, 256)
        mask = row16 == jnp.broadcast_to(code[0:1, :] >> 8, (16, 256))
        left = jnp.concatenate(
            [s_s[level, j, pl.ds(i * 128 + base, 16), :] for level in range(2) for j in range(4) for i in range(4)],
            axis=0,
        )
        both = dot(left, hot)
        total = both[:256] + both[256:]
        for c in range(CELLS):
            tg[spot, c : c + 1, :] = jnp.sum(
                jnp.where(mask, total[c * 16 : (c + 1) * 16, :], 0.0), axis=0, keepdims=True
            )
        return carry

    lax.fori_loop(0, BANDS, gather, 0, unroll=UNROLL)
    for half in range(2):
        pieces = []
        for eh in range(2):
            group = [tg[half * PAIRS + x, :, eh * 128 : (eh + 1) * 128] for x in range(4)]
            pieces += chunk_swap(group, lane16)
        turned = jnp.transpose(jnp.concatenate(pieces, axis=0))
        for x in range(PAIRS):
            base = pl.multiple_of(band_of(half * PAIRS + x) * BLOCKS, BLOCKS)
            out_ref[pl.ds(base, BLOCKS), :] = turned[x * BLOCKS : (x + 1) * BLOCKS, :]


def conv(strip, near, pair, psf):
    fwd, back, rfwd, rback = tables()
    any_spec = pl.BlockSpec(memory_space=pl.ANY)
    vmem_spec = pl.BlockSpec(memory_space=pltpu.VMEM)
    return pl.pallas_call(
        conv_kernel,
        out_shape=jax.ShapeDtypeStruct((BANDS * BLOCKS, 128), F32),
        in_specs=[
            pl.BlockSpec(memory_space=pltpu.SMEM), vmem_spec, vmem_spec,
            any_spec, any_spec, any_spec, any_spec, any_spec,
        ],
        out_specs=vmem_spec,
        scratch_shapes=[
            pltpu.VMEM((4, 1024, STRIP), BF),
            pltpu.VMEM((4, CHUNKS, 4 * STEP, 256), BF),
            pltpu.VMEM((2, L0, STRIP), F32),
            pltpu.VMEM((4, 512, 2 * PART0), BF),
            pltpu.VMEM((4, STRIP, 512), BF),
            pltpu.VMEM((BANDS, 3, CELLS, 256), F32),
            pltpu.VMEM((BANDS, 3, 8, 256), jnp.int32),
            pltpu.VMEM((2 * ROWS, 1024), BF),
            pltpu.VMEM((2 * ROWS, 1024), BF),
            pltpu.VMEM((2, 4, 256, STRIP), BF),
            pltpu.VMEM((CHUNKS, 4, 2 * STEP, STRIP), F32),
            pltpu.VMEM((2, 4, 2 * PART0, STRIP), BF),
            pltpu.VMEM((2, 2 * ROWS, STRIP), BF),
            pltpu.VMEM((2, 4, ROWS, 256), BF),
            pltpu.VMEM((BANDS, CELLS, 256), F32),
            pltpu.SemaphoreType.DMA((5,)),
        ],
        compiler_params=pltpu.CompilerParams(vmem_limit_bytes=VMEM_LIMIT),
        name="conv",
    )(strip, near, pair, jnp.asarray(fwd), jnp.asarray(rfwd), psf, jnp.asarray(rback), jnp.asarray(back))


def spread_kernel(meta_ref, back_ref, base_hbm, out_hbm, base, done, sems):
    loads, stores = [], []
    for i in range(4):
        lanes = pl.ds(i * 1024, 1024)
        loads.append(pltpu.make_async_copy(base_hbm.at[:, lanes], base.at[:, lanes], sems.at[i]))
        stores.append(pltpu.make_async_copy(done.at[:, lanes], out_hbm.at[:, lanes], sems.at[4 + i]))
    for load in loads:
        load.start()
    summed = back_ref[0:BLOCKS, :]
    for f in range(1, BANDS):
        summed = summed + back_ref[f * BLOCKS : (f + 1) * BLOCKS, :]
    meta = meta_ref[...]
    target, rank, right = meta[:, 0:1], meta[:, 1:2], meta[:, 2:3]
    hot = jnp.where(iota((SLOTS, BLOCKS), 1) == target, 1.0, 0.0).astype(BF)
    picked = jnp.zeros((SLOTS, 128), F32)
    for piece in split3(summed):
        picked = picked + dot(hot, piece)
    lane = iota((SLOTS, 128), 1)
    picked = jnp.where((lane >> 4) == rank, picked, 0.0)
    plain = jnp.where(right == 1, picked, 0.0)
    sides = split3(jnp.concatenate([plain, picked - plain], axis=1))
    krow, nlane = iota((256, 128), 0), iota((256, 128), 1)
    have_j = (krow >> 2) & 3
    have_j = jnp.where(krow >= 128, 3 - have_j, have_j)
    match = have_j == ((nlane >> 4) & 3)
    for i in range(4):
        weights = jnp.where(match & ((krow & 3) == i), 1.0, 0.0).astype(BF)
        value = dot(sides[0], weights) + (dot(sides[1], weights) + dot(sides[2], weights))
        loads[i].wait()
        for m in range(8):
            spot = slice(i * 1024 + m * 128, i * 1024 + (m + 1) * 128)
            done[:, spot] = (base[:, spot].astype(F32) + value).astype(BF)
        stores[i].start()
    for store in stores:
        store.wait()


def spread(meta, returned, base_grad):
    return pl.pallas_call(
        spread_kernel,
        out_shape=jax.ShapeDtypeStruct((SLOTS, 4096), BF),
        in_specs=[
            pl.BlockSpec(memory_space=pltpu.VMEM),
            pl.BlockSpec(memory_space=pltpu.VMEM),
            pl.BlockSpec(memory_space=pl.ANY),
        ],
        out_specs=pl.BlockSpec(memory_space=pl.ANY),
        scratch_shapes=[
            pltpu.VMEM((SLOTS, 4096), BF),
            pltpu.VMEM((SLOTS, 4096), BF),
            pltpu.SemaphoreType.DMA((8,)),
        ],
        compiler_params=pltpu.CompilerParams(vmem_limit_bytes=16 * 1024 * 1024),
        name="spread",
    )(meta, returned, base_grad)


def exchange(x, groups=None):
    return lax.all_to_all(
        x, ("fft", "tiles"), split_axis=0, concat_axis=0, axis_index_groups=groups, tiled=True
    )


def local(cotangent, base_grad, tile_place, tile_count, psf_spectrum):
    strip = lax.axis_index("fft").astype(jnp.int32).reshape(1, 1)
    message, meta = pool(cotangent, tile_place, tile_count)
    groups = [[f * BLOCKS + t for f in range(c, BANDS, 2) for t in range(BLOCKS)] for c in range(2)]
    near = exchange(message.reshape(PAIRS * BLOCKS, 4, 128), groups).reshape(-1, 128)
    pair = lax.ppermute(near, "fft", [(f, f ^ 1) for f in range(BANDS)])
    partial = conv(strip, near, pair, psf_spectrum)
    returned = exchange(partial)
    return spread(meta, returned, base_grad)


def solution(mesh):
    return jax.shard_map(
        local,
        mesh=mesh,
        in_specs=(
            P(("tiles", "fft"), None),
            P(("tiles", "fft"), None),
            P(("tiles", "fft")),
            P(("tiles", "fft")),
            P(None, None, "fft"),
        ),
        out_specs=P(("tiles", "fft"), None),
        check_vma=False,
    )
```

```python
import functools
import math

import jax
import jax.numpy as jnp
import ml_dtypes
import numpy as np
from jax import lax
from jax.experimental import pallas as pl
from jax.experimental.pallas import tpu as pltpu
from jax.sharding import PartitionSpec as P

BANDS = 8
BLOCKS = 32
BUCKET = 8
SLOTS = 256
SUB = 16
TCELL = 4
CELLS = 16
TILE_ROWS = 16
TILE_COLS = 256
ROWS = 512
L0 = 1536
L1 = 2048
STRIP = 256
HALF = 128
PART0 = L0 // 4
STEP = 128
CHUNKS = PART0 // STEP
PAIRS = BANDS // 2
BF = jnp.bfloat16
F32 = jnp.float32
UNROLL = 4
VMEM_LIMIT = 52 * 1024 * 1024


def split_np(table):
    high = table.astype(ml_dtypes.bfloat16)
    low = (table - high.astype(np.float64)).astype(ml_dtypes.bfloat16)
    return high, low


@functools.lru_cache(maxsize=None)
def tables():
    k = np.arange(L1)
    u = np.arange(L1 // 2).reshape(256, 4).T.reshape(-1)
    angle = (np.outer(2 * u + 1, k) % (2 * L1)) * (math.pi / L1)
    cos, sin = np.cos(angle), np.sin(angle)

    def strips(table):
        return table.reshape(table.shape[0], BANDS, STRIP).transpose(1, 0, 2)

    ch, cl = split_np(strips(cos))
    sh, sl = split_np(strips(-sin))
    fwd = np.stack([ch, cl, sh, sl], axis=1)
    near = (u < 2 * STRIP)
    scale = 1.0 / (L0 * L1)
    ch, cl = split_np(strips(cos[near]).transpose(0, 2, 1) * scale)
    sh, sl = split_np(strips(sin[near]).transpose(0, 2, 1) * scale)
    back = np.stack([ch, cl, sh, sl], axis=1)
    k0 = np.arange(PART0)
    rows = []
    for i in range(4):
        angle = (np.outer(k0, 4 * np.arange(128) + i) % L0) * (2 * math.pi / L0)
        c, s = np.cos(angle), np.sin(angle)
        rows.append(np.block([[c, s], [-s, c]]))
    rows = np.stack(rows)
    both = np.stack(split_np(rows)).reshape(2, 4, 2, CHUNKS, STEP, 256)
    rfwd = both.transpose(1, 0, 3, 2, 4, 5).reshape(4, 2, 2 * PART0, 256)
    rback = np.concatenate(split_np(rows.transpose(0, 2, 1)), axis=1)
    return fwd, back, rfwd, rback


def split(x):
    high = x.astype(BF)
    low = (x - high.astype(F32)).astype(BF)
    return high, low


def dot(a, b):
    return jnp.dot(a, b, preferred_element_type=F32)


def dot3(a_high, a_low, b_high, b_low):
    left = jnp.concatenate([a_high, a_high, a_low], axis=1)
    return dot(left, jnp.concatenate([b_high, b_low, b_high], axis=0))


def dot_nt(a, b):
    return lax.dot_general(a, b, (((1,), (1,)), ((), ())), preferred_element_type=F32)


def iota(shape, dim):
    return lax.broadcasted_iota(jnp.int32, shape, dim)


def pool_kernel(count_ref, place_hbm, cot_hbm, msg_ref, meta_ref, place_ref, cot, sems):
    fetch = pltpu.make_async_copy(place_hbm, place_ref, sems.at[4])
    fetch.start()
    copies = [
        pltpu.make_async_copy(
            cot_hbm.at[:, pl.ds(i * 1024, 1024)], cot.at[:, pl.ds(i * 1024, 1024)], sems.at[i]
        )
        for i in range(4)
    ]
    for copy in copies:
        copy.start()
    count = count_ref[0]
    fetch.wait()
    place_row = place_ref[...]
    square = (SLOTS, SLOTS)
    down, across = iota(square, 0), iota(square, 1)

    def fields(place, live):
        column = place & (BLOCKS * TILE_COLS - 1)
        row = (place >> 13) & (TILE_ROWS - 1)
        target = jnp.where(live, column >> 8, -8)
        return row, target, column & (TILE_COLS - 1)

    live_row = iota((1, SLOTS), 1) < count
    _, target_row, tc_row = fields(place_row, live_row)
    place_col = jnp.sum(
        jnp.where(down == across, place_row.astype(F32), 0.0), axis=1, keepdims=True
    ).astype(jnp.int32)
    live_col = iota((SLOTS, 1), 0) < count
    tr_col, target_col, tc_col = fields(place_col, live_col)
    before = (target_row == target_col) & (across < down) & live_row
    rank_col = jnp.sum(jnp.where(before, 1.0, 0.0), axis=1, keepdims=True).astype(jnp.int32)
    right_col = tc_col >= HALF
    lane = iota((SLOTS, 128), 1)
    meta_ref[...] = jnp.where(
        lane == 0, target_col, jnp.where(lane == 1, rank_col, right_col.astype(jnp.int32))
    )
    b = iota((BLOCKS, SLOTS), 0)
    right_row = tc_row >= HALF
    hot_own = target_row == b
    hot_left = (target_row == b - 1) & right_row & live_row
    hot_right = (target_row == b + 1) & (~right_row) & live_row
    hot = jnp.concatenate(
        [jnp.where(h, 1.0, 0.0) for h in (hot_own, hot_left, hot_right)], axis=0
    ).astype(BF)
    code_own = 1 + tr_col * 256 + jnp.where(right_col, tc_col - HALF, 255 - tc_col)
    code_halo = 1 + tr_col * 256 + jnp.where(right_col, 255 - tc_col, tc_col)
    mark_own = jnp.where(lane == rank_col, code_own, 0).astype(F32)
    mark_halo = jnp.where((lane & 7) == rank_col, code_halo, 0).astype(F32)
    prow, plane = iota((256, 256), 0), iota((256, 256), 1)
    want_j = (plane >> 2) & 3
    want_j = jnp.where(plane >= 128, 3 - want_j, want_j)
    match_j = ((prow >> 4) & 3) == want_j
    total = jnp.zeros((SLOTS, 256), F32)
    for i in range(4):
        weights = jnp.where(match_j & ((plane & 3) == i), 1.0, 0.0).astype(BF)
        copies[i].wait()
        total = total + dot(
            cot[:, i * 1024 : (i + 1) * 1024], jnp.concatenate([weights] * 4, axis=0)
        )
    plain, flipped = total[:, :128], total[:, 128:]
    here = (lane >> 4) == rank_col
    own = jnp.where(here, jnp.where(right_col, plain, flipped), 0.0)
    halo = jnp.where(here, jnp.where(right_col, flipped, plain), 0.0)
    loads = jnp.concatenate([own, halo, mark_own, mark_halo], axis=1)
    out = dot(jnp.concatenate([hot, hot], axis=1), jnp.concatenate(split(loads), axis=0))
    lane32 = iota((BLOCKS, 128), 1)
    marks = jnp.where(
        lane32 < 8,
        out[0:32, 256:384],
        jnp.where(lane32 < 16, out[32:64, 384:512], jnp.where(lane32 < 24, out[64:96, 384:512], 0.0)),
    )
    message = [out[0:32, 0:128], out[32:64, 128:256], out[64:96, 128:256], marks]
    for f in range(PAIRS):
        for a in range(4):
            msg_ref[pl.ds(f * BLOCKS * 4 + a, BLOCKS, stride=4), :] = message[a]


def pool(cotangent, tile_place, tile_count):
    return pl.pallas_call(
        pool_kernel,
        out_shape=(
            jax.ShapeDtypeStruct((PAIRS * BLOCKS * 4, 128), F32),
            jax.ShapeDtypeStruct((SLOTS, 128), jnp.int32),
        ),
        in_specs=[
            pl.BlockSpec(memory_space=pltpu.SMEM),
            pl.BlockSpec(memory_space=pltpu.HBM),
            pl.BlockSpec(memory_space=pltpu.HBM),
        ],
        out_specs=(
            pl.BlockSpec(memory_space=pltpu.VMEM),
            pl.BlockSpec(memory_space=pltpu.VMEM),
        ),
        scratch_shapes=[
            pltpu.VMEM((1, SLOTS), jnp.int32),
            pltpu.VMEM((SLOTS, 4096), BF),
            pltpu.SemaphoreType.DMA((5,)),
        ],
        compiler_params=pltpu.CompilerParams(vmem_limit_bytes=VMEM_LIMIT),
        name="pool",
    )(tile_count, tile_place.reshape(1, SLOTS), cotangent)


def chunk_swap(pieces, lane):
    out = []
    for band in range(4):
        value = None
        for e in range(4):
            moved = pieces[e] if e == band else pltpu.roll(pieces[e], ((e - band) * 32) % 128, 1)
            value = moved if value is None else jnp.where((lane >> 5) == e, moved, value)
        out.append(value)
    return out


def conv_kernel(
    f_ref, near_ref, pair_ref, fwd_hbm, rfwd_hbm, psf_hbm, rback_hbm, back_hbm, out_ref,
    fwd, rfwd, psf, rback, back, tv, tm, e_s, o_s, y_s, g_s, q_s, z_s, s_s, tg, sems,
):
    f = f_ref[0, 0]
    copies = [
        pltpu.make_async_copy(fwd_hbm.at[f], fwd, sems.at[0]),
        pltpu.make_async_copy(rfwd_hbm, rfwd, sems.at[1]),
        pltpu.make_async_copy(psf_hbm, psf, sems.at[2]),
        pltpu.make_async_copy(rback_hbm, rback, sems.at[3]),
        pltpu.make_async_copy(back_hbm.at[f], back, sems.at[4]),
    ]
    copies[0].start()
    core = f & 1

    lane16 = iota((16, 128), 1)
    lane8 = iota((8, 128), 1)
    for half, ref in enumerate((near_ref, pair_ref)):
        turned = [jnp.transpose(ref[pl.ds(a, 128, stride=4), :]) for a in range(4)]
        for nbr in range(3):
            for eh in range(2):
                group = [turned[nbr][(eh * 4 + e) * 16 : (eh * 4 + e + 1) * 16, :] for e in range(4)]
                for x, value in enumerate(chunk_swap(group, lane16)):
                    tv[half * PAIRS + x, nbr, :, eh * 128 : (eh + 1) * 128] = value
                marks = turned[3][nbr * 8 : nbr * 8 + 8, :]
                group = [
                    jnp.broadcast_to(marks[eh * 4 + e : eh * 4 + e + 1, :], (8, 128)) for e in range(4)
                ]
                for x, value in enumerate(chunk_swap(group, lane8)):
                    tm[half * PAIRS + x, nbr, :, eh * 128 : (eh + 1) * 128] = value.astype(jnp.int32) - 1

    row16 = iota((16, 256), 0)

    def band_of(spot):
        return 2 * (spot & (PAIRS - 1)) + (core ^ (spot >> 2))

    def hot_of(code, rows):
        place = jnp.broadcast_to(code[0:1, :] & 255, (rows, 256)).astype(jnp.int16)
        hit = iota((rows, 256), 0).astype(jnp.int16) == place
        return jnp.where(hit, jnp.ones((), BF), jnp.zeros((), BF))

    def scatter(spot, carry):
        base = pl.multiple_of(band_of(spot) * 16, 16)
        outs = []
        for nbr in range(3):
            code = tm[spot, nbr]
            mask = row16 == jnp.broadcast_to(code[0:1, :] >> 8, (16, 256))
            values = tv[spot, nbr]
            high = values.astype(BF).astype(F32)
            low = values - high
            sides = []
            for piece in (high, low):
                parts = [
                    jnp.where(mask, jnp.broadcast_to(piece[c : c + 1, :], (16, 256)), 0.0).astype(BF)
                    for c in range(CELLS)
                ]
                sides.append(jnp.concatenate(parts, axis=0))
            hot = hot_of(code, 256 if nbr == 0 else 128)
            outs.append(dot_nt(jnp.concatenate(sides, axis=1), jnp.concatenate([hot, hot], axis=1)))
        near_r, near_l = outs[0][:, :128], outs[0][:, 128:]
        far_l, far_r = outs[1], outs[2]
        for ref, near, far in ((e_s, near_r + near_l, far_r + far_l), (o_s, near_r - near_l, far_r - far_l)):
            for part, value in enumerate((near, far)):
                for level, piece in enumerate(split(value)):
                    for j in range(4):
                        for i in range(4):
                            ref[pl.ds(level * ROWS + i * 128 + base, 16),
                                j * 256 + part * 128 : j * 256 + (part + 1) * 128] = (
                                piece[(j * 4 + i) * 16 : (j * 4 + i + 1) * 16, :]
                            )
        return carry

    copies[1].start()
    copies[2].start()
    lax.fori_loop(0, BANDS, scatter, 0, unroll=UNROLL)
    copies[3].start()
    copies[4].start()

    copies[0].wait()
    for part, ref in enumerate((e_s, o_s)):
        y = dot3(ref[:ROWS, :], ref[ROWS:, :], fwd[2 * part], fwd[2 * part + 1])
        for level, piece in enumerate(split(y)):
            for i in range(4):
                y_s[level, i, part * 128 : (part + 1) * 128, :] = piece[i * 128 : (i + 1) * 128]

    copies[1].wait()
    copies[2].wait()

    def four(v, sign):
        (ar, ai), (br, bi), (cr, ci), (dr, di) = v
        pr, pi_, mr, mi = ar + cr, ai + ci, ar - cr, ai - ci
        qr, qi, nr, ni = br + dr, bi + di, br - dr, bi - di
        if sign > 0:
            return [(pr + qr, pi_ + qi), (mr - ni, mi + nr), (pr - qr, pi_ - qi), (mr + ni, mi - nr)]
        return [(pr + qr, pi_ + qi), (mr + ni, mi - nr), (pr - qr, pi_ - qi), (mr - ni, mi + nr)]

    for chunk in range(CHUNKS):
        for i in range(4):
            rows = slice(chunk * 2 * STEP, (chunk + 1) * 2 * STEP)
            g_s[chunk, i] = dot3(rfwd[i, 0, rows, :], rfwd[i, 1, rows, :], y_s[0, i], y_s[1, i])
        for r in range(0, STEP, 16):
            for lanes in (slice(0, 128), slice(128, 256)):
                g = [(g_s[chunk, i, r : r + 16, lanes], g_s[chunk, i, STEP + r : STEP + r + 16, lanes])
                     for i in range(4)]
                prod = []
                for m, (xr, xi) in enumerate(four(g, -1)):
                    rows = slice(m * PART0 + chunk * STEP + r, m * PART0 + chunk * STEP + r + 16)
                    hr, hi = psf[0, rows, lanes], psf[1, rows, lanes]
                    prod.append((xr * hr - xi * hi, xr * hi + xi * hr))
                for i, pair in enumerate(four(prod, 1)):
                    for part in range(2):
                        rows = slice(part * PART0 + chunk * STEP + r, part * PART0 + chunk * STEP + r + 16)
                        for level, piece in enumerate(split(pair[part])):
                            q_s[level, i, rows, lanes] = piece

    copies[3].wait()
    for i in range(4):
        z = dot3(rback[i, :256, :], rback[i, 256:, :], q_s[0, i], q_s[1, i])
        for level, piece in enumerate(split(z)):
            for part in range(2):
                z_s[part, level * ROWS + i * 128 : level * ROWS + (i + 1) * 128, :] = (
                    piece[part * 128 : (part + 1) * 128]
                )
    copies[4].wait()
    for jj in range(2):
        lanes = slice(jj * 256, (jj + 1) * 256)
        sums = []
        for part in range(2):
            sums.append(
                dot3(z_s[part, :ROWS, :], z_s[part, ROWS:, :], back[2 * part, :, lanes], back[2 * part + 1, :, lanes])
            )
        for side, value in enumerate((sums[0] - sums[1], sums[0] + sums[1])):
            for level, piece in enumerate(split(value)):
                for j in range(2):
                    s_s[level, 2 * jj + j, :, side * 128 : (side + 1) * 128] = (
                        piece[:, j * 128 : (j + 1) * 128]
                    )

    def gather(spot, carry):
        base = pl.multiple_of(band_of(spot) * 16, 16)
        code = tm[spot, 0]
        hot = hot_of(code, 256)
        mask = row16 == jnp.broadcast_to(code[0:1, :] >> 8, (16, 256))
        left = [
            jnp.concatenate(
                [s_s[level, j, pl.ds(i * 128 + base, 16), :] for j in range(4) for i in range(4)], axis=0
            )
            for level in range(2)
        ]
        total = dot(jnp.concatenate(left, axis=1), jnp.concatenate([hot, hot], axis=0))
        for c in range(CELLS):
            tg[spot, c : c + 1, :] = jnp.sum(
                jnp.where(mask, total[c * 16 : (c + 1) * 16, :], 0.0), axis=0, keepdims=True
            )
        return carry

    lax.fori_loop(0, BANDS, gather, 0, unroll=UNROLL)
    for half in range(2):
        pieces = []
        for eh in range(2):
            group = [tg[half * PAIRS + x, :, eh * 128 : (eh + 1) * 128] for x in range(4)]
            pieces += chunk_swap(group, lane16)
        turned = jnp.transpose(jnp.concatenate(pieces, axis=0))
        for x in range(PAIRS):
            base = pl.multiple_of(band_of(half * PAIRS + x) * BLOCKS, BLOCKS)
            out_ref[pl.ds(base, BLOCKS), :] = turned[x * BLOCKS : (x + 1) * BLOCKS, :]


def conv(strip, near, pair, psf):
    fwd, back, rfwd, rback = tables()
    any_spec = pl.BlockSpec(memory_space=pl.ANY)
    vmem_spec = pl.BlockSpec(memory_space=pltpu.VMEM)
    return pl.pallas_call(
        conv_kernel,
        out_shape=jax.ShapeDtypeStruct((BANDS * BLOCKS, 128), F32),
        in_specs=[
            pl.BlockSpec(memory_space=pltpu.SMEM), vmem_spec, vmem_spec,
            any_spec, any_spec, any_spec, any_spec, any_spec,
        ],
        out_specs=vmem_spec,
        scratch_shapes=[
            pltpu.VMEM((4, 1024, STRIP), BF),
            pltpu.VMEM((4, 2, 2 * PART0, 256), BF),
            pltpu.VMEM((2, L0, STRIP), F32),
            pltpu.VMEM((4, 512, 2 * PART0), BF),
            pltpu.VMEM((4, STRIP, 512), BF),
            pltpu.VMEM((BANDS, 3, CELLS, 256), F32),
            pltpu.VMEM((BANDS, 3, 8, 256), jnp.int32),
            pltpu.VMEM((2 * ROWS, 1024), BF),
            pltpu.VMEM((2 * ROWS, 1024), BF),
            pltpu.VMEM((2, 4, 256, STRIP), BF),
            pltpu.VMEM((CHUNKS, 4, 2 * STEP, STRIP), F32),
            pltpu.VMEM((2, 4, 2 * PART0, STRIP), BF),
            pltpu.VMEM((2, 2 * ROWS, STRIP), BF),
            pltpu.VMEM((2, 4, ROWS, 256), BF),
            pltpu.VMEM((BANDS, CELLS, 256), F32),
            pltpu.SemaphoreType.DMA((5,)),
        ],
        compiler_params=pltpu.CompilerParams(vmem_limit_bytes=VMEM_LIMIT),
        name="conv",
    )(strip, near, pair, jnp.asarray(fwd), jnp.asarray(rfwd), psf, jnp.asarray(rback), jnp.asarray(back))


def spread_kernel(meta_ref, back_ref, base_ref, out_hbm, done, sems):
    summed = back_ref[0:BLOCKS, :]
    for f in range(1, BANDS):
        summed = summed + back_ref[f * BLOCKS : (f + 1) * BLOCKS, :]
    meta = meta_ref[...]
    target, rank, right = meta[:, 0:1], meta[:, 1:2], meta[:, 2:3]
    lane64 = iota((SLOTS, 2 * BLOCKS), 1) & (BLOCKS - 1)
    hot = jnp.where(lane64 == target, 1.0, 0.0).astype(BF)
    picked = dot(hot, jnp.concatenate(split(summed), axis=0))
    lane = iota((SLOTS, 128), 1)
    picked = jnp.where((lane >> 4) == rank, picked, 0.0)
    plain = jnp.where(right == 1, picked, 0.0)
    sides = jnp.concatenate(split(plain) + split(picked - plain), axis=1)
    krow, nlane = iota((512, 128), 0), iota((512, 128), 1)
    have_j = (krow >> 2) & 3
    have_j = jnp.where(krow >= 256, 3 - have_j, have_j)
    match = have_j == ((nlane >> 4) & 3)
    stores = []
    for i in range(4):
        value = dot(sides, jnp.where(match & ((krow & 3) == i), 1.0, 0.0).astype(BF))
        for h in range(2):
            for m in range(4):
                at = i * 1024 + h * 512 + m * 128
                done[:, at : at + 128] = (base_ref[:, at : at + 128].astype(F32) + value).astype(BF)
            lanes = pl.ds(i * 1024 + h * 512, 512)
            stores.append(
                pltpu.make_async_copy(done.at[:, lanes], out_hbm.at[:, lanes], sems.at[2 * i + h])
            )
            stores[-1].start()
    for store in stores:
        store.wait()


def spread(meta, returned, base_grad):
    vmem_spec = pl.BlockSpec(memory_space=pltpu.VMEM)
    return pl.pallas_call(
        spread_kernel,
        out_shape=jax.ShapeDtypeStruct((SLOTS, 4096), BF),
        in_specs=[vmem_spec, vmem_spec, vmem_spec],
        out_specs=pl.BlockSpec(memory_space=pltpu.HBM),
        scratch_shapes=[pltpu.VMEM((SLOTS, 4096), BF), pltpu.SemaphoreType.DMA((8,))],
        compiler_params=pltpu.CompilerParams(vmem_limit_bytes=16 * 1024 * 1024),
        name="spread",
    )(meta, returned, base_grad)


def exchange(x, groups=None):
    return lax.all_to_all(
        x, ("fft", "tiles"), split_axis=0, concat_axis=0, axis_index_groups=groups, tiled=True
    )


def local(cotangent, base_grad, tile_place, tile_count, psf_spectrum):
    strip = lax.axis_index("fft").astype(jnp.int32).reshape(1, 1)
    message, meta = pool(cotangent, tile_place, tile_count)
    groups = [[f * BLOCKS + t for f in range(c, BANDS, 2) for t in range(BLOCKS)] for c in range(2)]
    near = exchange(message.reshape(PAIRS * BLOCKS, 4, 128), groups).reshape(-1, 128)
    pair = lax.ppermute(near, "fft", [(f, f ^ 1) for f in range(BANDS)])
    partial = conv(strip, near, pair, psf_spectrum)
    returned = exchange(partial)
    return spread(meta, returned, base_grad)


def solution(mesh):
    return jax.shard_map(
        local,
        mesh=mesh,
        in_specs=(
            P(("tiles", "fft"), None),
            P(("tiles", "fft"), None),
            P(("tiles", "fft")),
            P(("tiles", "fft")),
            P(None, None, "fft"),
        ),
        out_specs=P(("tiles", "fft"), None),
        check_vma=False,
    )
```

```python
import functools
import math

import jax
import jax.numpy as jnp
import ml_dtypes
import numpy as np
from jax import lax
from jax.experimental import pallas as pl
from jax.experimental.pallas import tpu as pltpu
from jax.sharding import PartitionSpec as P

BANDS = 8
BLOCKS = 32
BUCKET = 8
SLOTS = 256
SUB = 16
TCELL = 4
CELLS = 16
TILE_ROWS = 16
TILE_COLS = 256
ROWS = 512
L0 = 1536
L1 = 2048
STRIP = 256
HALF = 128
PART0 = L0 // 4
STEP = 128
CHUNKS = PART0 // STEP
PAIRS = BANDS // 2
BF = jnp.bfloat16
F32 = jnp.float32
VMEM_LIMIT = 48 * 1024 * 1024


def split_np(table):
    high = table.astype(ml_dtypes.bfloat16)
    low = (table - high.astype(np.float64)).astype(ml_dtypes.bfloat16)
    return high, low


@functools.lru_cache(maxsize=None)
def tables():
    k = np.arange(L1)
    u = np.arange(L1 // 2).reshape(256, 4).T.reshape(-1)
    angle = (np.outer(2 * u + 1, k) % (2 * L1)) * (math.pi / L1)
    cos, sin = np.cos(angle), np.sin(angle)

    def strips(table):
        return table.reshape(table.shape[0], BANDS, STRIP).transpose(1, 0, 2)

    ch, cl = split_np(strips(cos))
    sh, sl = split_np(strips(-sin))
    fwd = np.stack([ch, cl, sh, sl], axis=1)
    near = (u < 2 * STRIP)
    scale = 1.0 / (L0 * L1)
    ch, cl = split_np(strips(cos[near]).transpose(0, 2, 1) * scale)
    sh, sl = split_np(strips(sin[near]).transpose(0, 2, 1) * scale)
    back = np.stack([ch, cl, sh, sl], axis=1)
    k0 = np.arange(PART0)
    rfwd, rback = [], []
    for core in range(2):
        bands = np.r_[core:BANDS:2, 1 - core : BANDS : 2]
        tile_row = (bands[:, None] * TILE_ROWS + np.arange(TILE_ROWS)).reshape(-1)
        rows = []
        for i in range(4):
            angle = (np.outer(k0, 4 * tile_row + i) % L0) * (2 * math.pi / L0)
            c, s = np.cos(angle), np.sin(angle)
            rows.append(np.block([[c, s], [-s, c]]))
        rows = np.stack(rows)
        both = np.stack(split_np(rows)).reshape(2, 4, 2, CHUNKS, STEP, 256)
        rfwd.append(both.transpose(1, 0, 3, 2, 4, 5).reshape(4, 2, 2 * PART0, 256))
        rback.append(np.concatenate(split_np(rows.transpose(0, 2, 1)), axis=1))
    rfwd, rback = np.stack(rfwd), np.stack(rback)
    return fwd, back, rfwd, rback


def split(x):
    high = x.astype(BF)
    low = (x - high.astype(F32)).astype(BF)
    return high, low


def dot(a, b):
    return jnp.dot(a, b, preferred_element_type=F32)


def dot3(a_high, a_low, b_high, b_low):
    left = jnp.concatenate([a_high, a_high, a_low], axis=1)
    return dot(left, jnp.concatenate([b_high, b_low, b_high], axis=0))


def dot_nt(a, b):
    return lax.dot_general(a, b, (((1,), (1,)), ((), ())), preferred_element_type=F32)


def iota(shape, dim):
    return lax.broadcasted_iota(jnp.int32, shape, dim)


def pool_kernel(place_ref, cot_hbm, msg_ref, meta_ref, cot, sems):
    copies = [
        pltpu.make_async_copy(
            cot_hbm.at[:, pl.ds(i * 1024, 1024)], cot.at[:, pl.ds(i * 1024, 1024)], sems.at[i]
        )
        for i in range(4)
    ]
    for copy in copies:
        copy.start()
    place_row = place_ref[...]
    square = (SLOTS, SLOTS)
    down, across = iota(square, 0), iota(square, 1)

    def fields(place, live):
        column = place & (BLOCKS * TILE_COLS - 1)
        row = (place >> 13) & (TILE_ROWS - 1)
        target = jnp.where(live, column >> 8, -8)
        return row, target, column & (TILE_COLS - 1)

    live_row = place_row >= 0
    _, target_row, tc_row = fields(place_row, live_row)
    place_col = jnp.sum(
        jnp.where(down == across, place_row.astype(F32), 0.0), axis=1, keepdims=True
    ).astype(jnp.int32)
    live_col = place_col >= 0
    tr_col, target_col, tc_col = fields(place_col, live_col)
    before = (target_row == target_col) & (across < down) & live_row
    rank_col = jnp.sum(jnp.where(before, 1.0, 0.0), axis=1, keepdims=True).astype(jnp.int32)
    right_col = tc_col >= HALF
    lane = iota((SLOTS, 128), 1)
    meta_ref[...] = jnp.where(
        lane == 0, target_col, jnp.where(lane == 1, rank_col, right_col.astype(jnp.int32))
    )
    b = iota((BLOCKS, SLOTS), 0)
    right_row = tc_row >= HALF
    hot_own = target_row == b
    hot_left = (target_row == b - 1) & right_row & live_row
    hot_right = (target_row == b + 1) & (~right_row) & live_row
    hot = jnp.concatenate(
        [jnp.where(h, 1.0, 0.0) for h in (hot_own, hot_left, hot_right)], axis=0
    ).astype(BF)
    code_own = 1 + tr_col * 256 + jnp.where(right_col, tc_col - HALF, 255 - tc_col)
    code_halo = 1 + tr_col * 256 + jnp.where(right_col, 255 - tc_col, tc_col)
    mark_own = jnp.where(lane == rank_col, code_own, 0).astype(F32)
    mark_halo = jnp.where((lane & 7) == rank_col, code_halo, 0).astype(F32)
    prow, plane = iota((256, 256), 0), iota((256, 256), 1)
    want_j = (plane >> 2) & 3
    want_j = jnp.where(plane >= 128, 3 - want_j, want_j)
    match_j = ((prow >> 4) & 3) == want_j
    total = jnp.zeros((SLOTS, 256), F32)
    for i in range(4):
        weights = jnp.where(match_j & ((plane & 3) == i), 1.0, 0.0).astype(BF)
        copies[i].wait()
        total = total + dot(
            cot[:, i * 1024 : (i + 1) * 1024], jnp.concatenate([weights] * 4, axis=0)
        )
    plain, flipped = total[:, :128], total[:, 128:]
    here = (lane >> 4) == rank_col
    own = jnp.where(here, jnp.where(right_col, plain, flipped), 0.0)
    halo = jnp.where(here, jnp.where(right_col, flipped, plain), 0.0)
    loads = jnp.concatenate([own, halo, mark_own, mark_halo], axis=1)
    out = dot(jnp.concatenate([hot, hot], axis=1), jnp.concatenate(split(loads), axis=0))
    lane32 = iota((BLOCKS, 128), 1)
    marks = jnp.where(
        lane32 < 8,
        out[0:32, 256:384],
        jnp.where(lane32 < 16, out[32:64, 384:512], jnp.where(lane32 < 24, out[64:96, 384:512], 0.0)),
    )
    message = [out[0:32, 0:128], out[32:64, 128:256], out[64:96, 128:256], marks]
    for f in range(PAIRS):
        for a in range(4):
            msg_ref[pl.ds(f * BLOCKS * 4 + a, BLOCKS, stride=4), :] = message[a]


def pool(cotangent, tile_place, tile_count):
    live_place = jnp.where(jnp.arange(SLOTS, dtype=jnp.int32) < tile_count[0], tile_place, -1)
    return pl.pallas_call(
        pool_kernel,
        out_shape=(
            jax.ShapeDtypeStruct((PAIRS * BLOCKS * 4, 128), F32),
            jax.ShapeDtypeStruct((SLOTS, 128), jnp.int32),
        ),
        in_specs=[
            pl.BlockSpec(memory_space=pltpu.VMEM),
            pl.BlockSpec(memory_space=pl.ANY),
        ],
        out_specs=(
            pl.BlockSpec(memory_space=pltpu.VMEM),
            pl.BlockSpec(memory_space=pltpu.VMEM),
        ),
        scratch_shapes=[
            pltpu.VMEM((SLOTS, 4096), BF),
            pltpu.SemaphoreType.DMA((4,)),
        ],
        compiler_params=pltpu.CompilerParams(vmem_limit_bytes=VMEM_LIMIT),
        name="pool",
    )(live_place.reshape(1, SLOTS), cotangent)


def chunk_swap(pieces, lane):
    out = []
    for band in range(4):
        value = None
        for e in range(4):
            moved = pieces[e] if e == band else pltpu.roll(pieces[e], ((e - band) * 32) % 128, 1)
            value = moved if value is None else jnp.where((lane >> 5) == e, moved, value)
        out.append(value)
    return out


def arrive(ref, tv, tm):
    lane16 = iota((16, 128), 1)
    lane8 = iota((8, 128), 1)
    turned = [jnp.transpose(ref[pl.ds(a, 128, stride=4), :]) for a in range(4)]
    for nbr in range(3):
        for eh in range(2):
            group = [turned[nbr][(eh * 4 + e) * 16 : (eh * 4 + e + 1) * 16, :] for e in range(4)]
            for x, value in enumerate(chunk_swap(group, lane16)):
                tv[x, nbr, :, eh * 128 : (eh + 1) * 128] = value
            marks = turned[3][nbr * 8 : nbr * 8 + 8, :]
            group = [jnp.broadcast_to(marks[eh * 4 + e : eh * 4 + e + 1, :], (8, 128)) for e in range(4)]
            for x, value in enumerate(chunk_swap(group, lane8)):
                tm[x, nbr, :, eh * 128 : (eh + 1) * 128] = value.astype(jnp.int32) - 1


def hot_of(code, rows):
    place = jnp.broadcast_to(code[0:1, :] & 255, (rows, 256)).astype(jnp.int16)
    hit = iota((rows, 256), 0).astype(jnp.int16) == place
    return jnp.where(hit, jnp.ones((), BF), jnp.zeros((), BF))


def scatter(tv, tm, planes):
    row16 = iota((16, 256), 0)

    def one(x, carry):
        base = pl.multiple_of(x * 16, 16)
        outs = []
        for nbr in range(3):
            code = tm[x, nbr]
            mask = row16 == jnp.broadcast_to(code[0:1, :] >> 8, (16, 256))
            values = tv[x, nbr]
            high = values.astype(BF).astype(F32)
            low = values - high
            sides = []
            for piece in (high, low):
                parts = [
                    jnp.where(mask, jnp.broadcast_to(piece[c : c + 1, :], (16, 256)), 0.0).astype(BF)
                    for c in range(CELLS)
                ]
                sides.append(jnp.concatenate(parts, axis=0))
            hot = hot_of(code, 256 if nbr == 0 else 128)
            outs.append(dot_nt(jnp.concatenate(sides, axis=1), jnp.concatenate([hot, hot], axis=1)))
        near_r, near_l = outs[0][:, :128], outs[0][:, 128:]
        far_l, far_r = outs[1], outs[2]
        for kind, near, far in ((0, near_r + near_l, far_r + far_l), (1, near_r - near_l, far_r - far_l)):
            for part, value in enumerate((near, far)):
                for level, piece in enumerate(split(value)):
                    for j in range(4):
                        for i in range(4):
                            planes[kind, pl.ds(level * 256 + i * 64 + base, 16),
                                   j * 256 + part * 128 : j * 256 + (part + 1) * 128] = (
                                piece[(j * 4 + i) * 16 : (j * 4 + i + 1) * 16, :]
                            )
        return carry

    lax.fori_loop(0, PAIRS, one, 0, unroll=PAIRS)


def first_kernel(near_ref, planes_ref, codes_ref, tv, tm):
    arrive(near_ref, tv, tm)
    codes_ref[...] = tm[:, 0]
    scatter(tv, tm, planes_ref)


def first(near):
    vmem_spec = pl.BlockSpec(memory_space=pltpu.VMEM)
    return pl.pallas_call(
        first_kernel,
        out_shape=(
            jax.ShapeDtypeStruct((2, ROWS, 1024), BF),
            jax.ShapeDtypeStruct((PAIRS, 8, 256), jnp.int32),
        ),
        in_specs=[vmem_spec],
        out_specs=(vmem_spec, vmem_spec),
        scratch_shapes=[
            pltpu.VMEM((PAIRS, 3, CELLS, 256), F32),
            pltpu.VMEM((PAIRS, 3, 8, 256), jnp.int32),
        ],
        compiler_params=pltpu.CompilerParams(vmem_limit_bytes=16 * 1024 * 1024),
        cost_estimate=pl.CostEstimate(flops=2 * 10**9, bytes_accessed=4 * 10**6, transcendentals=0),
        name="first",
    )(near)


def conv_kernel(
    planes_ref, codes_ref, pair_ref, fwd_hbm, rfwd_hbm, psf_hbm, rback_hbm, back_hbm, out_ref,
    fwd, rfwd, psf, rback, back, tv, tm, planes, y_s, g_s, q_s, z_s, s_s, tg, sems,
):
    f = lax.axis_index("fft")
    core = f & 1
    copies = [
        pltpu.make_async_copy(fwd_hbm.at[f], fwd, sems.at[0]),
        pltpu.make_async_copy(rfwd_hbm.at[core], rfwd, sems.at[1]),
        pltpu.make_async_copy(psf_hbm, psf, sems.at[2]),
        pltpu.make_async_copy(rback_hbm.at[core], rback, sems.at[3]),
        pltpu.make_async_copy(back_hbm.at[f], back, sems.at[4]),
    ]
    copies[0].start()
    arrive(pair_ref, tv, tm)
    copies[1].start()
    copies[2].start()
    scatter(tv, tm, planes)
    copies[3].start()
    copies[4].start()

    copies[0].wait()
    for part in range(2):
        high, low = [
            jnp.concatenate([ref[part, level * 256 : (level + 1) * 256, :] for ref in (planes_ref, planes)], axis=0)
            for level in range(2)
        ]
        y = dot3(high, low, fwd[2 * part], fwd[2 * part + 1])
        for level, piece in enumerate(split(y)):
            for i in range(4):
                for half in range(2):
                    at = part * 128 + half * 64
                    y_s[level, i, at : at + 64, :] = piece[half * 256 + i * 64 : half * 256 + (i + 1) * 64]

    copies[1].wait()
    copies[2].wait()

    def four(v, sign):
        (ar, ai), (br, bi), (cr, ci), (dr, di) = v
        pr, pi_, mr, mi = ar + cr, ai + ci, ar - cr, ai - ci
        qr, qi, nr, ni = br + dr, bi + di, br - dr, bi - di
        if sign > 0:
            return [(pr + qr, pi_ + qi), (mr - ni, mi + nr), (pr - qr, pi_ - qi), (mr + ni, mi - nr)]
        return [(pr + qr, pi_ + qi), (mr + ni, mi - nr), (pr - qr, pi_ - qi), (mr - ni, mi + nr)]

    for chunk in range(CHUNKS):
        for i in range(4):
            rows = slice(chunk * 2 * STEP, (chunk + 1) * 2 * STEP)
            g_s[chunk, i] = dot3(rfwd[i, 0, rows, :], rfwd[i, 1, rows, :], y_s[0, i], y_s[1, i])
        for r in range(0, STEP, 16):
            for lanes in (slice(0, 128), slice(128, 256)):
                g = [(g_s[chunk, i, r : r + 16, lanes], g_s[chunk, i, STEP + r : STEP + r + 16, lanes])
                     for i in range(4)]
                prod = []
                for m, (xr, xi) in enumerate(four(g, -1)):
                    rows = slice(m * PART0 + chunk * STEP + r, m * PART0 + chunk * STEP + r + 16)
                    hr, hi = psf[0, rows, lanes], psf[1, rows, lanes]
                    prod.append((xr * hr - xi * hi, xr * hi + xi * hr))
                for i, pair in enumerate(four(prod, 1)):
                    for part in range(2):
                        rows = slice(part * PART0 + chunk * STEP + r, part * PART0 + chunk * STEP + r + 16)
                        for level, piece in enumerate(split(pair[part])):
                            q_s[level, i, rows, lanes] = piece

    copies[3].wait()
    for i in range(4):
        z = dot3(rback[i, :256, :], rback[i, 256:, :], q_s[0, i], q_s[1, i])
        for level, piece in enumerate(split(z)):
            for part in range(2):
                z_s[part, level * ROWS + i * 128 : level * ROWS + (i + 1) * 128, :] = (
                    piece[part * 128 : (part + 1) * 128]
                )
    copies[4].wait()
    for jj in range(2):
        lanes = slice(jj * 256, (jj + 1) * 256)
        sums = []
        for part in range(2):
            sums.append(
                dot3(z_s[part, :ROWS, :], z_s[part, ROWS:, :], back[2 * part, :, lanes], back[2 * part + 1, :, lanes])
            )
        for side, value in enumerate((sums[0] - sums[1], sums[0] + sums[1])):
            for level, piece in enumerate(split(value)):
                for j in range(2):
                    s_s[level, 2 * jj + j, :, side * 128 : (side + 1) * 128] = (
                        piece[:, j * 128 : (j + 1) * 128]
                    )

    row16 = iota((16, 256), 0)
    for half in range(2):

        def gather(x, carry, half=half):
            base = pl.multiple_of(half * 64 + x * 16, 16)
            code = codes_ref[x] if half == 0 else tm[x, 0]
            hot = hot_of(code, 256)
            mask = row16 == jnp.broadcast_to(code[0:1, :] >> 8, (16, 256))
            left = [
                jnp.concatenate(
                    [s_s[level, j, pl.ds(i * 128 + base, 16), :] for j in range(4) for i in range(4)], axis=0
                )
                for level in range(2)
            ]
            total = dot(jnp.concatenate(left, axis=1), jnp.concatenate([hot, hot], axis=0))
            for c in range(CELLS):
                tg[half, x, c : c + 1, :] = jnp.sum(
                    jnp.where(mask, total[c * 16 : (c + 1) * 16, :], 0.0), axis=0, keepdims=True
                )
            return carry

        lax.fori_loop(0, PAIRS, gather, 0, unroll=PAIRS)

    lane16 = iota((16, 128), 1)
    for half in range(2):
        pieces = []
        for eh in range(2):
            group = [tg[half, x, :, eh * 128 : (eh + 1) * 128] for x in range(4)]
            pieces += chunk_swap(group, lane16)
        turned = jnp.transpose(jnp.concatenate(pieces, axis=0))
        for x in range(PAIRS):
            base = pl.multiple_of((2 * x + (core ^ half)) * BLOCKS, BLOCKS)
            out_ref[pl.ds(base, BLOCKS), :] = turned[x * BLOCKS : (x + 1) * BLOCKS, :]


def conv(planes, codes, pair, psf):
    fwd, back, rfwd, rback = tables()
    any_spec = pl.BlockSpec(memory_space=pl.ANY)
    vmem_spec = pl.BlockSpec(memory_space=pltpu.VMEM)
    return pl.pallas_call(
        conv_kernel,
        out_shape=jax.ShapeDtypeStruct((BANDS * BLOCKS, 128), F32),
        in_specs=[
            vmem_spec, vmem_spec, vmem_spec,
            any_spec, any_spec, any_spec, any_spec, any_spec,
        ],
        out_specs=vmem_spec,
        scratch_shapes=[
            pltpu.VMEM((4, 1024, STRIP), BF),
            pltpu.VMEM((4, 2, 2 * PART0, 256), BF),
            pltpu.VMEM((2, L0, STRIP), F32),
            pltpu.VMEM((4, 512, 2 * PART0), BF),
            pltpu.VMEM((4, STRIP, 512), BF),
            pltpu.VMEM((PAIRS, 3, CELLS, 256), F32),
            pltpu.VMEM((PAIRS, 3, 8, 256), jnp.int32),
            pltpu.VMEM((2, ROWS, 1024), BF),
            pltpu.VMEM((2, 4, 256, STRIP), BF),
            pltpu.VMEM((CHUNKS, 4, 2 * STEP, STRIP), F32),
            pltpu.VMEM((2, 4, 2 * PART0, STRIP), BF),
            pltpu.VMEM((2, 2 * ROWS, STRIP), BF),
            pltpu.VMEM((2, 4, ROWS, 256), BF),
            pltpu.VMEM((2, PAIRS, CELLS, 256), F32),
            pltpu.SemaphoreType.DMA((5,)),
        ],
        compiler_params=pltpu.CompilerParams(vmem_limit_bytes=VMEM_LIMIT),
        name="conv",
    )(planes, codes, pair, jnp.asarray(fwd), jnp.asarray(rfwd), psf, jnp.asarray(rback), jnp.asarray(back))


def spread_kernel(meta_ref, back_ref, base_ref, out_hbm, done, sems):
    summed = back_ref[0:BLOCKS, :]
    for f in range(1, BANDS):
        summed = summed + back_ref[f * BLOCKS : (f + 1) * BLOCKS, :]
    meta = meta_ref[...]
    target, rank, right = meta[:, 0:1], meta[:, 1:2], meta[:, 2:3]
    lane64 = iota((SLOTS, 2 * BLOCKS), 1) & (BLOCKS - 1)
    hot = jnp.where(lane64 == target, 1.0, 0.0).astype(BF)
    picked = dot(hot, jnp.concatenate(split(summed), axis=0))
    lane = iota((SLOTS, 128), 1)
    picked = jnp.where((lane >> 4) == rank, picked, 0.0)
    plain = jnp.where(right == 1, picked, 0.0)
    sides = jnp.concatenate(split(plain) + split(picked - plain), axis=1)
    krow, nlane = iota((512, 128), 0), iota((512, 128), 1)
    have_j = (krow >> 2) & 3
    have_j = jnp.where(krow >= 256, 3 - have_j, have_j)
    match = have_j == ((nlane >> 4) & 3)
    stores = []
    for i in range(4):
        value = dot(sides, jnp.where(match & ((krow & 3) == i), 1.0, 0.0).astype(BF))
        for h in range(2):
            for m in range(4):
                at = i * 1024 + h * 512 + m * 128
                done[:, at : at + 128] = (base_ref[:, at : at + 128].astype(F32) + value).astype(BF)
            lanes = pl.ds(i * 1024 + h * 512, 512)
            stores.append(
                pltpu.make_async_copy(done.at[:, lanes], out_hbm.at[:, lanes], sems.at[2 * i + h])
            )
            stores[-1].start()
    for store in stores:
        store.wait()


def spread(meta, returned, base_grad):
    vmem_spec = pl.BlockSpec(memory_space=pltpu.VMEM)
    return pl.pallas_call(
        spread_kernel,
        out_shape=jax.ShapeDtypeStruct((SLOTS, 4096), BF),
        in_specs=[vmem_spec, vmem_spec, vmem_spec],
        out_specs=pl.BlockSpec(memory_space=pltpu.HBM),
        scratch_shapes=[pltpu.VMEM((SLOTS, 4096), BF), pltpu.SemaphoreType.DMA((8,))],
        compiler_params=pltpu.CompilerParams(vmem_limit_bytes=16 * 1024 * 1024),
        name="spread",
    )(meta, returned, base_grad)


def exchange(x, groups=None):
    return lax.all_to_all(
        x, ("fft", "tiles"), split_axis=0, concat_axis=0, axis_index_groups=groups, tiled=True
    )


def local(cotangent, base_grad, tile_place, tile_count, psf_spectrum):
    message, meta = pool(cotangent, tile_place, tile_count)
    groups = [[f * BLOCKS + t for f in range(c, BANDS, 2) for t in range(BLOCKS)] for c in range(2)]
    near = exchange(message.reshape(PAIRS * BLOCKS, 4, 128), groups).reshape(-1, 128)
    pair = lax.ppermute(near, "fft", [(f, f ^ 1) for f in range(BANDS)])
    planes, codes = first(near)
    partial = conv(planes, codes, pair, psf_spectrum)
    returned = exchange(partial)
    return spread(meta, returned, base_grad)


def solution(mesh):
    return jax.shard_map(
        local,
        mesh=mesh,
        in_specs=(
            P(("tiles", "fft"), None),
            P(("tiles", "fft"), None),
            P(("tiles", "fft")),
            P(("tiles", "fft")),
            P(None, None, "fft"),
        ),
        out_specs=P(("tiles", "fft"), None),
        check_vma=False,
    )
```

```python
import functools
import math

import jax
import jax.numpy as jnp
import ml_dtypes
import numpy as np
from jax import lax
from jax.experimental import pallas as pl
from jax.experimental.pallas import tpu as pltpu
from jax.sharding import PartitionSpec as P

BANDS = 8
BLOCKS = 32
BUCKET = 8
SLOTS = 256
SUB = 16
TCELL = 4
CELLS = 16
TILE_ROWS = 16
TILE_COLS = 256
ROWS = 512
L0 = 1536
L1 = 2048
STRIP = 256
HALF = 128
PART0 = L0 // 4
STEP = 128
CHUNKS = PART0 // STEP
PAIRS = BANDS // 2
BF = jnp.bfloat16
F32 = jnp.float32
VMEM_LIMIT = 52 * 1024 * 1024
CONV_VMEM_LIMIT = 48 * 1024 * 1024


def split_np(table):
    high = table.astype(ml_dtypes.bfloat16)
    low = (table - high.astype(np.float64)).astype(ml_dtypes.bfloat16)
    return high, low


@functools.lru_cache(maxsize=None)
def tables():
    k = np.arange(L1)
    u = np.arange(L1 // 2).reshape(256, 4).T.reshape(-1)
    angle = (np.outer(2 * u + 1, k) % (2 * L1)) * (math.pi / L1)
    cos, sin = np.cos(angle), np.sin(angle)

    def strips(table):
        return table.reshape(table.shape[0], BANDS, STRIP).transpose(1, 0, 2)

    ch, cl = split_np(strips(cos))
    sh, sl = split_np(strips(-sin))
    fwd = np.stack([ch, cl, sh, sl], axis=1)
    near = (u < 2 * STRIP)
    scale = 1.0 / (L0 * L1)
    ch, cl = split_np(strips(cos[near]).transpose(0, 2, 1) * scale)
    sh, sl = split_np(strips(sin[near]).transpose(0, 2, 1) * scale)
    back = np.stack([ch, cl, sh, sl], axis=1)
    k0 = np.arange(PART0)
    rfwd, rback = [], []
    for core in range(2):
        bands = np.r_[core:BANDS:2, 1 - core : BANDS : 2]
        tile_row = (bands[:, None] * TILE_ROWS + np.arange(TILE_ROWS)).reshape(-1)
        rows = []
        for i in range(4):
            angle = (np.outer(k0, 4 * tile_row + i) % L0) * (2 * math.pi / L0)
            c, s = np.cos(angle), np.sin(angle)
            rows.append(np.block([[c, s], [-s, c]]))
        rows = np.stack(rows)
        both = np.stack(split_np(rows)).reshape(2, 4, 2, CHUNKS, STEP, 256)
        rfwd.append(both.transpose(1, 0, 3, 2, 4, 5).reshape(4, 2, 2 * PART0, 256))
        rback.append(np.concatenate(split_np(rows.transpose(0, 2, 1)), axis=1))
    rfwd, rback = np.stack(rfwd), np.stack(rback)
    return fwd, back, rfwd, rback


def split(x):
    high = x.astype(BF)
    low = (x - high.astype(F32)).astype(BF)
    return high, low


def dot(a, b):
    return jnp.dot(a, b, preferred_element_type=F32)


def dot3(a_high, a_low, b_high, b_low):
    left = jnp.concatenate([a_high, a_high, a_low], axis=1)
    return dot(left, jnp.concatenate([b_high, b_low, b_high], axis=0))


def dot_nt(a, b):
    return lax.dot_general(a, b, (((1,), (1,)), ((), ())), preferred_element_type=F32)


def iota(shape, dim):
    return lax.broadcasted_iota(jnp.int32, shape, dim)


def pool_kernel(place_ref, cot_hbm, msg_ref, meta_ref, cot, sems):
    copies = [
        pltpu.make_async_copy(
            cot_hbm.at[:, pl.ds(i * 1024, 1024)], cot.at[:, pl.ds(i * 1024, 1024)], sems.at[i]
        )
        for i in range(4)
    ]
    for copy in copies:
        copy.start()
    place_row = place_ref[...]
    square = (SLOTS, SLOTS)
    down, across = iota(square, 0), iota(square, 1)

    def fields(place, live):
        column = place & (BLOCKS * TILE_COLS - 1)
        row = (place >> 13) & (TILE_ROWS - 1)
        target = jnp.where(live, column >> 8, -8)
        return row, target, column & (TILE_COLS - 1)

    live_row = place_row >= 0
    _, target_row, tc_row = fields(place_row, live_row)
    place_col = jnp.sum(
        jnp.where(down == across, place_row.astype(F32), 0.0), axis=1, keepdims=True
    ).astype(jnp.int32)
    live_col = place_col >= 0
    tr_col, target_col, tc_col = fields(place_col, live_col)
    before = (target_row == target_col) & (across < down) & live_row
    rank_col = jnp.sum(jnp.where(before, 1.0, 0.0), axis=1, keepdims=True).astype(jnp.int32)
    right_col = tc_col >= HALF
    lane = iota((SLOTS, 128), 1)
    meta_ref[...] = jnp.where(
        lane == 0, target_col, jnp.where(lane == 1, rank_col, right_col.astype(jnp.int32))
    )
    b = iota((BLOCKS, SLOTS), 0)
    right_row = tc_row >= HALF
    hot_own = target_row == b
    hot_left = (target_row == b - 1) & right_row & live_row
    hot_right = (target_row == b + 1) & (~right_row) & live_row
    hot = jnp.concatenate(
        [jnp.where(h, 1.0, 0.0) for h in (hot_own, hot_left, hot_right)], axis=0
    ).astype(BF)
    code_own = 1 + tr_col * 256 + jnp.where(right_col, tc_col - HALF, 255 - tc_col)
    code_halo = 1 + tr_col * 256 + jnp.where(right_col, 255 - tc_col, tc_col)
    mark_own = jnp.where(lane == rank_col, code_own, 0).astype(F32)
    mark_halo = jnp.where((lane & 7) == rank_col, code_halo, 0).astype(F32)
    prow, plane = iota((256, 256), 0), iota((256, 256), 1)
    want_j = (plane >> 2) & 3
    want_j = jnp.where(plane >= 128, 3 - want_j, want_j)
    match_j = ((prow >> 4) & 3) == want_j
    total = jnp.zeros((SLOTS, 256), F32)
    for i in range(4):
        weights = jnp.where(match_j & ((plane & 3) == i), 1.0, 0.0).astype(BF)
        copies[i].wait()
        total = total + dot(
            cot[:, i * 1024 : (i + 1) * 1024], jnp.concatenate([weights] * 4, axis=0)
        )
    plain, flipped = total[:, :128], total[:, 128:]
    here = (lane >> 4) == rank_col
    own = jnp.where(here, jnp.where(right_col, plain, flipped), 0.0)
    halo = jnp.where(here, jnp.where(right_col, flipped, plain), 0.0)
    loads = jnp.concatenate([own, halo, mark_own, mark_halo], axis=1)
    out = dot(jnp.concatenate([hot, hot], axis=1), jnp.concatenate(split(loads), axis=0))
    lane32 = iota((BLOCKS, 128), 1)
    marks = jnp.where(
        lane32 < 8,
        out[0:32, 256:384],
        jnp.where(lane32 < 16, out[32:64, 384:512], jnp.where(lane32 < 24, out[64:96, 384:512], 0.0)),
    )
    message = [out[0:32, 0:128], out[32:64, 128:256], out[64:96, 128:256], marks]
    for f in range(PAIRS):
        for a in range(4):
            msg_ref[pl.ds(f * BLOCKS * 4 + a, BLOCKS, stride=4), :] = message[a]


def pool(cotangent, tile_place, tile_count):
    live_place = jnp.where(jnp.arange(SLOTS, dtype=jnp.int32) < tile_count[0], tile_place, -1)
    return pl.pallas_call(
        pool_kernel,
        out_shape=(
            jax.ShapeDtypeStruct((PAIRS * BLOCKS * 4, 128), F32),
            jax.ShapeDtypeStruct((SLOTS, 128), jnp.int32),
        ),
        in_specs=[
            pl.BlockSpec(memory_space=pltpu.VMEM),
            pl.BlockSpec(memory_space=pl.ANY),
        ],
        out_specs=(
            pl.BlockSpec(memory_space=pltpu.VMEM),
            pl.BlockSpec(memory_space=pltpu.VMEM),
        ),
        scratch_shapes=[
            pltpu.VMEM((SLOTS, 4096), BF),
            pltpu.SemaphoreType.DMA((4,)),
        ],
        compiler_params=pltpu.CompilerParams(vmem_limit_bytes=VMEM_LIMIT),
        name="pool",
    )(live_place.reshape(1, SLOTS), cotangent)


def chunk_swap(pieces, lane):
    out = []
    for band in range(4):
        value = None
        for e in range(4):
            moved = pieces[e] if e == band else pltpu.roll(pieces[e], ((e - band) * 32) % 128, 1)
            value = moved if value is None else jnp.where((lane >> 5) == e, moved, value)
        out.append(value)
    return out


def arrive(ref, tv, tm):
    lane16 = iota((16, 128), 1)
    lane8 = iota((8, 128), 1)
    turned = [jnp.transpose(ref[pl.ds(a, 128, stride=4), :]) for a in range(4)]
    for nbr in range(3):
        for eh in range(2):
            group = [turned[nbr][(eh * 4 + e) * 16 : (eh * 4 + e + 1) * 16, :] for e in range(4)]
            for x, value in enumerate(chunk_swap(group, lane16)):
                tv[x, nbr, :, eh * 128 : (eh + 1) * 128] = value
            marks = turned[3][nbr * 8 : nbr * 8 + 8, :]
            group = [jnp.broadcast_to(marks[eh * 4 + e : eh * 4 + e + 1, :], (8, 128)) for e in range(4)]
            for x, value in enumerate(chunk_swap(group, lane8)):
                tm[x, nbr, :, eh * 128 : (eh + 1) * 128] = value.astype(jnp.int32) - 1


def hot_of(code, rows):
    place = jnp.broadcast_to(code[0:1, :] & 255, (rows, 256)).astype(jnp.int16)
    hit = iota((rows, 256), 0).astype(jnp.int16) == place
    return jnp.where(hit, jnp.ones((), BF), jnp.zeros((), BF))


def scatter(tv, tm, planes):
    row16 = iota((16, 256), 0)

    def one(x, carry):
        base = pl.multiple_of(x * 16, 16)
        outs = []
        for nbr in range(3):
            code = tm[x, nbr]
            mask = row16 == jnp.broadcast_to(code[0:1, :] >> 8, (16, 256))
            values = tv[x, nbr]
            high = values.astype(BF).astype(F32)
            low = values - high
            sides = []
            for piece in (high, low):
                parts = [
                    jnp.where(mask, jnp.broadcast_to(piece[c : c + 1, :], (16, 256)), 0.0).astype(BF)
                    for c in range(CELLS)
                ]
                sides.append(jnp.concatenate(parts, axis=0))
            hot = hot_of(code, 256 if nbr == 0 else 128)
            outs.append(dot_nt(jnp.concatenate(sides, axis=1), jnp.concatenate([hot, hot], axis=1)))
        near_r, near_l = outs[0][:, :128], outs[0][:, 128:]
        far_l, far_r = outs[1], outs[2]
        for kind, near, far in ((0, near_r + near_l, far_r + far_l), (1, near_r - near_l, far_r - far_l)):
            for part, value in enumerate((near, far)):
                for level, piece in enumerate(split(value)):
                    for j in range(4):
                        for i in range(4):
                            planes[kind, pl.ds(level * 256 + i * 64 + base, 16),
                                   j * 256 + part * 128 : j * 256 + (part + 1) * 128] = (
                                piece[(j * 4 + i) * 16 : (j * 4 + i + 1) * 16, :]
                            )
        return carry

    lax.fori_loop(0, PAIRS, one, 0, unroll=PAIRS)


def first_kernel(near_ref, planes_ref, codes_ref, tv, tm):
    arrive(near_ref, tv, tm)
    codes_ref[...] = tm[:, 0]
    scatter(tv, tm, planes_ref)


def first(near):
    vmem_spec = pl.BlockSpec(memory_space=pltpu.VMEM)
    return pl.pallas_call(
        first_kernel,
        out_shape=(
            jax.ShapeDtypeStruct((2, ROWS, 1024), BF),
            jax.ShapeDtypeStruct((PAIRS, 8, 256), jnp.int32),
        ),
        in_specs=[vmem_spec],
        out_specs=(vmem_spec, vmem_spec),
        scratch_shapes=[
            pltpu.VMEM((PAIRS, 3, CELLS, 256), F32),
            pltpu.VMEM((PAIRS, 3, 8, 256), jnp.int32),
        ],
        compiler_params=pltpu.CompilerParams(vmem_limit_bytes=16 * 1024 * 1024),
        cost_estimate=pl.CostEstimate(flops=2 * 10**9, bytes_accessed=4 * 10**6, transcendentals=0),
        name="first",
    )(near)


def conv_kernel(
    planes_ref, codes_ref, pair_ref, fwd_hbm, rfwd_hbm, psf_hbm, rback_hbm, back_hbm, out_ref,
    fwd, rfwd, psf, rback, back, tv, tm, planes, y_s, g_s, q_s, z_s, s_s, tg, sems,
):
    f = lax.axis_index("fft")
    core = f & 1
    copies = [
        pltpu.make_async_copy(fwd_hbm.at[f], fwd, sems.at[0]),
        pltpu.make_async_copy(rfwd_hbm.at[core], rfwd, sems.at[1]),
        pltpu.make_async_copy(psf_hbm, psf, sems.at[2]),
        pltpu.make_async_copy(rback_hbm.at[core], rback, sems.at[3]),
        pltpu.make_async_copy(back_hbm.at[f], back, sems.at[4]),
    ]
    copies[0].start()
    arrive(pair_ref, tv, tm)
    copies[1].start()
    copies[2].start()
    scatter(tv, tm, planes)
    copies[3].start()
    copies[4].start()

    copies[0].wait()
    for part in range(2):
        high, low = [
            jnp.concatenate([ref[part, level * 256 : (level + 1) * 256, :] for ref in (planes_ref, planes)], axis=0)
            for level in range(2)
        ]
        y = dot3(high, low, fwd[2 * part], fwd[2 * part + 1])
        for level, piece in enumerate(split(y)):
            for i in range(4):
                for half in range(2):
                    at = part * 128 + half * 64
                    y_s[level, i, at : at + 64, :] = piece[half * 256 + i * 64 : half * 256 + (i + 1) * 64]

    copies[1].wait()
    copies[2].wait()

    def four(v, sign):
        (ar, ai), (br, bi), (cr, ci), (dr, di) = v
        pr, pi_, mr, mi = ar + cr, ai + ci, ar - cr, ai - ci
        qr, qi, nr, ni = br + dr, bi + di, br - dr, bi - di
        if sign > 0:
            return [(pr + qr, pi_ + qi), (mr - ni, mi + nr), (pr - qr, pi_ - qi), (mr + ni, mi - nr)]
        return [(pr + qr, pi_ + qi), (mr + ni, mi - nr), (pr - qr, pi_ - qi), (mr - ni, mi + nr)]

    for chunk in range(CHUNKS):
        for i in range(4):
            rows = slice(chunk * 2 * STEP, (chunk + 1) * 2 * STEP)
            g_s[chunk, i] = dot3(rfwd[i, 0, rows, :], rfwd[i, 1, rows, :], y_s[0, i], y_s[1, i])
        for r in range(0, STEP, 16):
            for lanes in (slice(0, 128), slice(128, 256)):
                g = [(g_s[chunk, i, r : r + 16, lanes], g_s[chunk, i, STEP + r : STEP + r + 16, lanes])
                     for i in range(4)]
                prod = []
                for m, (xr, xi) in enumerate(four(g, -1)):
                    rows = slice(m * PART0 + chunk * STEP + r, m * PART0 + chunk * STEP + r + 16)
                    hr, hi = psf[0, rows, lanes], psf[1, rows, lanes]
                    prod.append((xr * hr - xi * hi, xr * hi + xi * hr))
                for i, pair in enumerate(four(prod, 1)):
                    for part in range(2):
                        rows = slice(part * PART0 + chunk * STEP + r, part * PART0 + chunk * STEP + r + 16)
                        for level, piece in enumerate(split(pair[part])):
                            q_s[level, i, rows, lanes] = piece

    copies[3].wait()
    for i in range(4):
        z = dot3(rback[i, :256, :], rback[i, 256:, :], q_s[0, i], q_s[1, i])
        for level, piece in enumerate(split(z)):
            for part in range(2):
                z_s[part, level * ROWS + i * 128 : level * ROWS + (i + 1) * 128, :] = (
                    piece[part * 128 : (part + 1) * 128]
                )
    copies[4].wait()
    for jj in range(2):
        lanes = slice(jj * 256, (jj + 1) * 256)
        sums = []
        for part in range(2):
            sums.append(
                dot3(z_s[part, :ROWS, :], z_s[part, ROWS:, :], back[2 * part, :, lanes], back[2 * part + 1, :, lanes])
            )
        for side, value in enumerate((sums[0] - sums[1], sums[0] + sums[1])):
            for level, piece in enumerate(split(value)):
                for j in range(2):
                    s_s[level, 2 * jj + j, :, side * 128 : (side + 1) * 128] = (
                        piece[:, j * 128 : (j + 1) * 128]
                    )

    row16 = iota((16, 256), 0)
    for half in range(2):

        def gather(x, carry, half=half):
            base = pl.multiple_of(half * 64 + x * 16, 16)
            code = codes_ref[x] if half == 0 else tm[x, 0]
            hot = hot_of(code, 256)
            mask = row16 == jnp.broadcast_to(code[0:1, :] >> 8, (16, 256))
            left = [
                jnp.concatenate(
                    [s_s[level, j, pl.ds(i * 128 + base, 16), :] for j in range(4) for i in range(4)], axis=0
                )
                for level in range(2)
            ]
            total = dot(jnp.concatenate(left, axis=1), jnp.concatenate([hot, hot], axis=0))
            for c in range(CELLS):
                tg[half, x, c : c + 1, :] = jnp.sum(
                    jnp.where(mask, total[c * 16 : (c + 1) * 16, :], 0.0), axis=0, keepdims=True
                )
            return carry

        lax.fori_loop(0, PAIRS, gather, 0, unroll=PAIRS)

    lane16 = iota((16, 128), 1)
    for half in range(2):
        pieces = []
        for eh in range(2):
            group = [tg[half, x, :, eh * 128 : (eh + 1) * 128] for x in range(4)]
            pieces += chunk_swap(group, lane16)
        turned = jnp.transpose(jnp.concatenate(pieces, axis=0))
        for x in range(PAIRS):
            base = pl.multiple_of((2 * x + (core ^ half)) * BLOCKS, BLOCKS)
            out_ref[pl.ds(base, BLOCKS), :] = turned[x * BLOCKS : (x + 1) * BLOCKS, :]


def conv(planes, codes, pair, psf):
    fwd, back, rfwd, rback = tables()
    any_spec = pl.BlockSpec(memory_space=pl.ANY)
    vmem_spec = pl.BlockSpec(memory_space=pltpu.VMEM)
    return pl.pallas_call(
        conv_kernel,
        out_shape=jax.ShapeDtypeStruct((BANDS * BLOCKS, 128), F32),
        in_specs=[
            vmem_spec, vmem_spec, vmem_spec,
            any_spec, any_spec, any_spec, any_spec, any_spec,
        ],
        out_specs=vmem_spec,
        scratch_shapes=[
            pltpu.VMEM((4, 1024, STRIP), BF),
            pltpu.VMEM((4, 2, 2 * PART0, 256), BF),
            pltpu.VMEM((2, L0, STRIP), F32),
            pltpu.VMEM((4, 512, 2 * PART0), BF),
            pltpu.VMEM((4, STRIP, 512), BF),
            pltpu.VMEM((PAIRS, 3, CELLS, 256), F32),
            pltpu.VMEM((PAIRS, 3, 8, 256), jnp.int32),
            pltpu.VMEM((2, ROWS, 1024), BF),
            pltpu.VMEM((2, 4, 256, STRIP), BF),
            pltpu.VMEM((CHUNKS, 4, 2 * STEP, STRIP), F32),
            pltpu.VMEM((2, 4, 2 * PART0, STRIP), BF),
            pltpu.VMEM((2, 2 * ROWS, STRIP), BF),
            pltpu.VMEM((2, 4, ROWS, 256), BF),
            pltpu.VMEM((2, PAIRS, CELLS, 256), F32),
            pltpu.SemaphoreType.DMA((5,)),
        ],
        compiler_params=pltpu.CompilerParams(vmem_limit_bytes=CONV_VMEM_LIMIT),
        name="conv",
    )(planes, codes, pair, jnp.asarray(fwd), jnp.asarray(rfwd), psf, jnp.asarray(rback), jnp.asarray(back))


def spread_kernel(meta_ref, back_ref, base_ref, out_hbm, done, sems):
    summed = back_ref[0:BLOCKS, :]
    for f in range(1, BANDS):
        summed = summed + back_ref[f * BLOCKS : (f + 1) * BLOCKS, :]
    meta = meta_ref[...]
    target, rank, right = meta[:, 0:1], meta[:, 1:2], meta[:, 2:3]
    lane64 = iota((SLOTS, 2 * BLOCKS), 1) & (BLOCKS - 1)
    hot = jnp.where(lane64 == target, 1.0, 0.0).astype(BF)
    picked = dot(hot, jnp.concatenate(split(summed), axis=0))
    lane = iota((SLOTS, 128), 1)
    picked = jnp.where((lane >> 4) == rank, picked, 0.0)
    plain = jnp.where(right == 1, picked, 0.0)
    sides = jnp.concatenate(split(plain) + split(picked - plain), axis=1)
    krow, nlane = iota((512, 128), 0), iota((512, 128), 1)
    have_j = (krow >> 2) & 3
    have_j = jnp.where(krow >= 256, 3 - have_j, have_j)
    match = have_j == ((nlane >> 4) & 3)
    stores = []
    for i in range(4):
        value = dot(sides, jnp.where(match & ((krow & 3) == i), 1.0, 0.0).astype(BF))
        for h in range(2):
            for m in range(4):
                at = i * 1024 + h * 512 + m * 128
                done[:, at : at + 128] = (base_ref[:, at : at + 128].astype(F32) + value).astype(BF)
            lanes = pl.ds(i * 1024 + h * 512, 512)
            stores.append(
                pltpu.make_async_copy(done.at[:, lanes], out_hbm.at[:, lanes], sems.at[2 * i + h])
            )
            stores[-1].start()
    for store in stores:
        store.wait()


def spread(meta, returned, base_grad):
    vmem_spec = pl.BlockSpec(memory_space=pltpu.VMEM)
    return pl.pallas_call(
        spread_kernel,
        out_shape=jax.ShapeDtypeStruct((SLOTS, 4096), BF),
        in_specs=[vmem_spec, vmem_spec, vmem_spec],
        out_specs=pl.BlockSpec(memory_space=pltpu.HBM),
        scratch_shapes=[pltpu.VMEM((SLOTS, 4096), BF), pltpu.SemaphoreType.DMA((8,))],
        compiler_params=pltpu.CompilerParams(vmem_limit_bytes=16 * 1024 * 1024),
        name="spread",
    )(meta, returned, base_grad)


def exchange(x, groups=None):
    return lax.all_to_all(
        x, ("fft", "tiles"), split_axis=0, concat_axis=0, axis_index_groups=groups, tiled=True
    )


def local(cotangent, base_grad, tile_place, tile_count, psf_spectrum):
    message, meta = pool(cotangent, tile_place, tile_count)
    groups = [[f * BLOCKS + t for f in range(c, BANDS, 2) for t in range(BLOCKS)] for c in range(2)]
    near = exchange(message.reshape(PAIRS * BLOCKS, 4, 128), groups).reshape(-1, 128)
    pair = lax.ppermute(near, "fft", [(f, f ^ 1) for f in range(BANDS)])
    planes, codes = first(near)
    partial = conv(planes, codes, pair, psf_spectrum)
    returned = exchange(partial)
    return spread(meta, returned, base_grad)


def solution(mesh):
    return jax.shard_map(
        local,
        mesh=mesh,
        in_specs=(
            P(("tiles", "fft"), None),
            P(("tiles", "fft"), None),
            P(("tiles", "fft")),
            P(("tiles", "fft")),
            P(None, None, "fft"),
        ),
        out_specs=P(("tiles", "fft"), None),
        check_vma=False,
    )
```

```python
import functools
import math

import jax
import jax.numpy as jnp
import ml_dtypes
import numpy as np
from jax import lax
from jax.experimental import pallas as pl
from jax.experimental.pallas import tpu as pltpu
from jax.sharding import PartitionSpec as P

BANDS = 8
BLOCKS = 32
BUCKET = 8
SLOTS = 256
SUB = 16
TCELL = 4
CELLS = 16
TILE_ROWS = 16
TILE_COLS = 256
ROWS = 512
L0 = 1536
L1 = 2048
STRIP = 256
HALF = 128
PART0 = L0 // 4
STEP = 128
CHUNKS = PART0 // STEP
PAIRS = BANDS // 2
BF = jnp.bfloat16
F32 = jnp.float32
VMEM_LIMIT = 52 * 1024 * 1024
CONV_VMEM_LIMIT = 47 * 1024 * 1024


def split_np(table):
    high = table.astype(ml_dtypes.bfloat16)
    low = (table - high.astype(np.float64)).astype(ml_dtypes.bfloat16)
    return high, low


@functools.lru_cache(maxsize=None)
def tables():
    k = np.arange(L1)
    u = np.arange(L1 // 2).reshape(256, 4).T.reshape(-1)
    angle = (np.outer(2 * u + 1, k) % (2 * L1)) * (math.pi / L1)
    cos, sin = np.cos(angle), np.sin(angle)

    def strips(table):
        return table.reshape(table.shape[0], BANDS, STRIP).transpose(1, 0, 2)

    ch, cl = split_np(strips(cos))
    sh, sl = split_np(strips(-sin))
    fwd = np.stack([ch, cl, sh, sl], axis=1)
    near = (u < 2 * STRIP)
    scale = 1.0 / (L0 * L1)
    ch, cl = split_np(strips(cos[near]).transpose(0, 2, 1) * scale)
    sh, sl = split_np(strips(sin[near]).transpose(0, 2, 1) * scale)
    back = np.stack([ch, cl, sh, sl], axis=1)
    k0 = np.arange(PART0)
    rfwd, rback = [], []
    for core in range(2):
        bands = np.r_[core:BANDS:2, 1 - core : BANDS : 2]
        tile_row = (bands[:, None] * TILE_ROWS + np.arange(TILE_ROWS)).reshape(-1)
        rows = []
        for i in range(4):
            angle = (np.outer(k0, 4 * tile_row + i) % L0) * (2 * math.pi / L0)
            c, s = np.cos(angle), np.sin(angle)
            rows.append(np.block([[c, s], [-s, c]]))
        rows = np.stack(rows)
        both = np.stack(split_np(rows)).reshape(2, 4, 2, CHUNKS, STEP, 256)
        rfwd.append(both.transpose(1, 0, 3, 2, 4, 5).reshape(4, 2, 2 * PART0, 256))
        rback.append(np.concatenate(split_np(rows.transpose(0, 2, 1)), axis=1))
    rfwd, rback = np.stack(rfwd), np.stack(rback)
    return fwd, back, rfwd, rback


def split(x):
    high = x.astype(BF)
    low = (x - high.astype(F32)).astype(BF)
    return high, low


def dot(a, b):
    return jnp.dot(a, b, preferred_element_type=F32)


def dot3(a_high, a_low, b_high, b_low):
    left = jnp.concatenate([a_high, a_high, a_low], axis=1)
    return dot(left, jnp.concatenate([b_high, b_low, b_high], axis=0))


def dot_nt(a, b):
    return lax.dot_general(a, b, (((1,), (1,)), ((), ())), preferred_element_type=F32)


def iota(shape, dim):
    return lax.broadcasted_iota(jnp.int32, shape, dim)


def pool_kernel(place_ref, cot_hbm, msg_ref, meta_ref, cot, sems):
    copies = [
        pltpu.make_async_copy(
            cot_hbm.at[:, pl.ds(i * 1024, 1024)], cot.at[:, pl.ds(i * 1024, 1024)], sems.at[i]
        )
        for i in range(4)
    ]
    for copy in copies:
        copy.start()
    place_row = place_ref[...]
    square = (SLOTS, SLOTS)
    down, across = iota(square, 0), iota(square, 1)

    def fields(place, live):
        column = place & (BLOCKS * TILE_COLS - 1)
        row = (place >> 13) & (TILE_ROWS - 1)
        target = jnp.where(live, column >> 8, -8)
        return row, target, column & (TILE_COLS - 1)

    live_row = place_row >= 0
    _, target_row, tc_row = fields(place_row, live_row)
    place_col = jnp.sum(
        jnp.where(down == across, place_row.astype(F32), 0.0), axis=1, keepdims=True
    ).astype(jnp.int32)
    live_col = place_col >= 0
    tr_col, target_col, tc_col = fields(place_col, live_col)
    before = (target_row == target_col) & (across < down) & live_row
    rank_col = jnp.sum(jnp.where(before, 1.0, 0.0), axis=1, keepdims=True).astype(jnp.int32)
    right_col = tc_col >= HALF
    lane = iota((SLOTS, 128), 1)
    meta_ref[...] = jnp.where(
        lane == 0, target_col, jnp.where(lane == 1, rank_col, right_col.astype(jnp.int32))
    )
    b = iota((BLOCKS, SLOTS), 0)
    right_row = tc_row >= HALF
    hot_own = target_row == b
    hot_left = (target_row == b - 1) & right_row & live_row
    hot_right = (target_row == b + 1) & (~right_row) & live_row
    hot = jnp.concatenate(
        [jnp.where(h, 1.0, 0.0) for h in (hot_own, hot_left, hot_right)], axis=0
    ).astype(BF)
    code_own = 1 + tr_col * 256 + jnp.where(right_col, tc_col - HALF, 255 - tc_col)
    code_halo = 1 + tr_col * 256 + jnp.where(right_col, 255 - tc_col, tc_col)
    mark_own = jnp.where(lane == rank_col, code_own, 0).astype(F32)
    mark_halo = jnp.where((lane & 7) == rank_col, code_halo, 0).astype(F32)
    prow, plane = iota((256, 256), 0), iota((256, 256), 1)
    want_j = (plane >> 2) & 3
    want_j = jnp.where(plane >= 128, 3 - want_j, want_j)
    match_j = ((prow >> 4) & 3) == want_j
    total = jnp.zeros((SLOTS, 256), F32)
    for i in range(4):
        weights = jnp.where(match_j & ((plane & 3) == i), 1.0, 0.0).astype(BF)
        copies[i].wait()
        total = total + dot(
            cot[:, i * 1024 : (i + 1) * 1024], jnp.concatenate([weights] * 4, axis=0)
        )
    plain, flipped = total[:, :128], total[:, 128:]
    here = (lane >> 4) == rank_col
    own = jnp.where(here, jnp.where(right_col, plain, flipped), 0.0)
    halo = jnp.where(here, jnp.where(right_col, flipped, plain), 0.0)
    loads = jnp.concatenate([own, halo, mark_own, mark_halo], axis=1)
    out = dot(jnp.concatenate([hot, hot], axis=1), jnp.concatenate(split(loads), axis=0))
    lane32 = iota((BLOCKS, 128), 1)
    marks = jnp.where(
        lane32 < 8,
        out[0:32, 256:384],
        jnp.where(lane32 < 16, out[32:64, 384:512], jnp.where(lane32 < 24, out[64:96, 384:512], 0.0)),
    )
    message = [out[0:32, 0:128], out[32:64, 128:256], out[64:96, 128:256], marks]
    for f in range(PAIRS):
        for a in range(4):
            msg_ref[pl.ds(f * BLOCKS * 4 + a, BLOCKS, stride=4), :] = message[a]


def pool(cotangent, tile_place, tile_count):
    live_place = jnp.where(jnp.arange(SLOTS, dtype=jnp.int32) < tile_count[0], tile_place, -1)
    return pl.pallas_call(
        pool_kernel,
        out_shape=(
            jax.ShapeDtypeStruct((PAIRS * BLOCKS * 4, 128), F32),
            jax.ShapeDtypeStruct((SLOTS, 128), jnp.int32),
        ),
        in_specs=[
            pl.BlockSpec(memory_space=pltpu.VMEM),
            pl.BlockSpec(memory_space=pl.ANY),
        ],
        out_specs=(
            pl.BlockSpec(memory_space=pltpu.VMEM),
            pl.BlockSpec(memory_space=pltpu.VMEM),
        ),
        scratch_shapes=[
            pltpu.VMEM((SLOTS, 4096), BF),
            pltpu.SemaphoreType.DMA((4,)),
        ],
        compiler_params=pltpu.CompilerParams(vmem_limit_bytes=VMEM_LIMIT),
        name="pool",
    )(live_place.reshape(1, SLOTS), cotangent)


def chunk_swap(pieces, lane):
    out = []
    for band in range(4):
        value = None
        for e in range(4):
            moved = pieces[e] if e == band else pltpu.roll(pieces[e], ((e - band) * 32) % 128, 1)
            value = moved if value is None else jnp.where((lane >> 5) == e, moved, value)
        out.append(value)
    return out


def arrive(ref, tv, tm):
    lane16 = iota((16, 128), 1)
    lane8 = iota((8, 128), 1)
    turned = [jnp.transpose(ref[pl.ds(a, 128, stride=4), :]) for a in range(4)]
    for nbr in range(3):
        for eh in range(2):
            group = [turned[nbr][(eh * 4 + e) * 16 : (eh * 4 + e + 1) * 16, :] for e in range(4)]
            for x, value in enumerate(chunk_swap(group, lane16)):
                tv[x, nbr, :, eh * 128 : (eh + 1) * 128] = value
            marks = turned[3][nbr * 8 : nbr * 8 + 8, :]
            group = [jnp.broadcast_to(marks[eh * 4 + e : eh * 4 + e + 1, :], (8, 128)) for e in range(4)]
            for x, value in enumerate(chunk_swap(group, lane8)):
                tm[x, nbr, :, eh * 128 : (eh + 1) * 128] = value.astype(jnp.int32) - 1


def hot_of(code, rows):
    place = jnp.broadcast_to(code[0:1, :] & 255, (rows, 256)).astype(jnp.int16)
    hit = iota((rows, 256), 0).astype(jnp.int16) == place
    return jnp.where(hit, jnp.ones((), BF), jnp.zeros((), BF))


def scatter(tv, tm, planes, hots):
    row16 = iota((16, 256), 0)

    def one(x, carry):
        base = pl.multiple_of(x * 16, 16)
        outs = []
        for nbr in range(3):
            code = tm[x, nbr]
            mask = row16 == jnp.broadcast_to(code[0:1, :] >> 8, (16, 256))
            values = tv[x, nbr]
            high = values.astype(BF).astype(F32)
            low = values - high
            sides = []
            for piece in (high, low):
                parts = [
                    jnp.where(mask, jnp.broadcast_to(piece[c : c + 1, :], (16, 256)), 0.0).astype(BF)
                    for c in range(CELLS)
                ]
                sides.append(jnp.concatenate(parts, axis=0))
            hot = hot_of(code, 256 if nbr == 0 else 128)
            if nbr == 0:
                hots[x] = hot
            outs.append(dot_nt(jnp.concatenate(sides, axis=1), jnp.concatenate([hot, hot], axis=1)))
        near_r, near_l = outs[0][:, :128], outs[0][:, 128:]
        far_l, far_r = outs[1], outs[2]
        for kind, near, far in ((0, near_r + near_l, far_r + far_l), (1, near_r - near_l, far_r - far_l)):
            for part, value in enumerate((near, far)):
                for level, piece in enumerate(split(value)):
                    for j in range(4):
                        for i in range(4):
                            planes[kind, pl.ds(level * 256 + i * 64 + base, 16),
                                   j * 256 + part * 128 : j * 256 + (part + 1) * 128] = (
                                piece[(j * 4 + i) * 16 : (j * 4 + i + 1) * 16, :]
                            )
        return carry

    lax.fori_loop(0, PAIRS, one, 0, unroll=PAIRS)


def first_kernel(near_ref, planes_ref, codes_ref, hots_ref, tv, tm):
    arrive(near_ref, tv, tm)
    codes_ref[...] = tm[:, 0]
    scatter(tv, tm, planes_ref, hots_ref)


def first(near):
    vmem_spec = pl.BlockSpec(memory_space=pltpu.VMEM)
    return pl.pallas_call(
        first_kernel,
        out_shape=(
            jax.ShapeDtypeStruct((2, ROWS, 1024), BF),
            jax.ShapeDtypeStruct((PAIRS, 8, 256), jnp.int32),
            jax.ShapeDtypeStruct((PAIRS, 256, 256), BF),
        ),
        in_specs=[vmem_spec],
        out_specs=(vmem_spec, vmem_spec, vmem_spec),
        scratch_shapes=[
            pltpu.VMEM((PAIRS, 3, CELLS, 256), F32),
            pltpu.VMEM((PAIRS, 3, 8, 256), jnp.int32),
        ],
        compiler_params=pltpu.CompilerParams(vmem_limit_bytes=16 * 1024 * 1024),
        cost_estimate=pl.CostEstimate(flops=2 * 10**9, bytes_accessed=4 * 10**6, transcendentals=0),
        name="first",
    )(near)


def conv_kernel(
    planes_ref, codes_ref, hots_ref, pair_ref, fwd_hbm, rfwd_hbm, psf_hbm, rback_hbm, back_hbm, out_ref,
    fwd, rfwd, psf, rback, back, tv, tm, planes, hots, y_s, g_s, q_s, z_s, s_s, tg, sems,
):
    f = lax.axis_index("fft")
    core = f & 1
    copies = [
        pltpu.make_async_copy(fwd_hbm.at[f], fwd, sems.at[0]),
        pltpu.make_async_copy(rfwd_hbm.at[core], rfwd, sems.at[1]),
        pltpu.make_async_copy(psf_hbm, psf, sems.at[2]),
        pltpu.make_async_copy(rback_hbm.at[core], rback, sems.at[3]),
        pltpu.make_async_copy(back_hbm.at[f], back, sems.at[4]),
    ]
    copies[0].start()
    arrive(pair_ref, tv, tm)
    copies[1].start()
    copies[2].start()
    scatter(tv, tm, planes, hots)
    copies[3].start()
    copies[4].start()

    copies[0].wait()
    for part in range(2):
        high, low = [
            jnp.concatenate([ref[part, level * 256 : (level + 1) * 256, :] for ref in (planes_ref, planes)], axis=0)
            for level in range(2)
        ]
        y = dot3(high, low, fwd[2 * part], fwd[2 * part + 1])
        for level, piece in enumerate(split(y)):
            for i in range(4):
                for half in range(2):
                    at = part * 128 + half * 64
                    y_s[level, i, at : at + 64, :] = piece[half * 256 + i * 64 : half * 256 + (i + 1) * 64]

    copies[1].wait()
    copies[2].wait()

    def four(v, sign):
        (ar, ai), (br, bi), (cr, ci), (dr, di) = v
        pr, pi_, mr, mi = ar + cr, ai + ci, ar - cr, ai - ci
        qr, qi, nr, ni = br + dr, bi + di, br - dr, bi - di
        if sign > 0:
            return [(pr + qr, pi_ + qi), (mr - ni, mi + nr), (pr - qr, pi_ - qi), (mr + ni, mi - nr)]
        return [(pr + qr, pi_ + qi), (mr + ni, mi - nr), (pr - qr, pi_ - qi), (mr - ni, mi + nr)]

    for chunk in range(CHUNKS):
        for i in range(4):
            rows = slice(chunk * 2 * STEP, (chunk + 1) * 2 * STEP)
            g_s[chunk, i] = dot3(rfwd[i, 0, rows, :], rfwd[i, 1, rows, :], y_s[0, i], y_s[1, i])
        for r in range(0, STEP, 16):
            for lanes in (slice(0, 128), slice(128, 256)):
                g = [(g_s[chunk, i, r : r + 16, lanes], g_s[chunk, i, STEP + r : STEP + r + 16, lanes])
                     for i in range(4)]
                prod = []
                for m, (xr, xi) in enumerate(four(g, -1)):
                    rows = slice(m * PART0 + chunk * STEP + r, m * PART0 + chunk * STEP + r + 16)
                    hr, hi = psf[0, rows, lanes], psf[1, rows, lanes]
                    prod.append((xr * hr - xi * hi, xr * hi + xi * hr))
                for i, pair in enumerate(four(prod, 1)):
                    for part in range(2):
                        rows = slice(part * PART0 + chunk * STEP + r, part * PART0 + chunk * STEP + r + 16)
                        for level, piece in enumerate(split(pair[part])):
                            q_s[level, i, rows, lanes] = piece

    copies[3].wait()
    for i in range(4):
        z = dot3(rback[i, :256, :], rback[i, 256:, :], q_s[0, i], q_s[1, i])
        for level, piece in enumerate(split(z)):
            for part in range(2):
                z_s[part, level * ROWS + i * 128 : level * ROWS + (i + 1) * 128, :] = (
                    piece[part * 128 : (part + 1) * 128]
                )
    copies[4].wait()
    for jj in range(2):
        lanes = slice(jj * 256, (jj + 1) * 256)
        sums = []
        for part in range(2):
            sums.append(
                dot3(z_s[part, :ROWS, :], z_s[part, ROWS:, :], back[2 * part, :, lanes], back[2 * part + 1, :, lanes])
            )
        for side, value in enumerate((sums[0] - sums[1], sums[0] + sums[1])):
            for level, piece in enumerate(split(value)):
                for j in range(2):
                    s_s[level, 2 * jj + j, :, side * 128 : (side + 1) * 128] = (
                        piece[:, j * 128 : (j + 1) * 128]
                    )

    row16 = iota((16, 256), 0)
    for half in range(2):

        def gather(x, carry, half=half):
            base = pl.multiple_of(half * 64 + x * 16, 16)
            code = codes_ref[x] if half == 0 else tm[x, 0]
            hot = hots_ref[x] if half == 0 else hots[x]
            mask = row16 == jnp.broadcast_to(code[0:1, :] >> 8, (16, 256))
            left = [
                jnp.concatenate(
                    [s_s[level, j, pl.ds(i * 128 + base, 16), :] for j in range(4) for i in range(4)], axis=0
                )
                for level in range(2)
            ]
            total = dot(jnp.concatenate(left, axis=1), jnp.concatenate([hot, hot], axis=0))
            for c in range(CELLS):
                tg[half, x, c : c + 1, :] = jnp.sum(
                    jnp.where(mask, total[c * 16 : (c + 1) * 16, :], 0.0), axis=0, keepdims=True
                )
            return carry

        lax.fori_loop(0, PAIRS, gather, 0, unroll=PAIRS)

    lane16 = iota((16, 128), 1)
    for half in range(2):
        pieces = []
        for eh in range(2):
            group = [tg[half, x, :, eh * 128 : (eh + 1) * 128] for x in range(4)]
            pieces += chunk_swap(group, lane16)
        turned = jnp.transpose(jnp.concatenate(pieces, axis=0))
        for x in range(PAIRS):
            base = pl.multiple_of((2 * x + (core ^ half)) * BLOCKS, BLOCKS)
            out_ref[pl.ds(base, BLOCKS), :] = turned[x * BLOCKS : (x + 1) * BLOCKS, :]


def conv(planes, codes, hots, pair, psf):
    fwd, back, rfwd, rback = tables()
    any_spec = pl.BlockSpec(memory_space=pl.ANY)
    vmem_spec = pl.BlockSpec(memory_space=pltpu.VMEM)
    return pl.pallas_call(
        conv_kernel,
        out_shape=jax.ShapeDtypeStruct((BANDS * BLOCKS, 128), F32),
        in_specs=[
            vmem_spec, vmem_spec, vmem_spec, vmem_spec,
            any_spec, any_spec, any_spec, any_spec, any_spec,
        ],
        out_specs=vmem_spec,
        scratch_shapes=[
            pltpu.VMEM((4, 1024, STRIP), BF),
            pltpu.VMEM((4, 2, 2 * PART0, 256), BF),
            pltpu.VMEM((2, L0, STRIP), F32),
            pltpu.VMEM((4, 512, 2 * PART0), BF),
            pltpu.VMEM((4, STRIP, 512), BF),
            pltpu.VMEM((PAIRS, 3, CELLS, 256), F32),
            pltpu.VMEM((PAIRS, 3, 8, 256), jnp.int32),
            pltpu.VMEM((2, ROWS, 1024), BF),
            pltpu.VMEM((PAIRS, 256, 256), BF),
            pltpu.VMEM((2, 4, 256, STRIP), BF),
            pltpu.VMEM((CHUNKS, 4, 2 * STEP, STRIP), F32),
            pltpu.VMEM((2, 4, 2 * PART0, STRIP), BF),
            pltpu.VMEM((2, 2 * ROWS, STRIP), BF),
            pltpu.VMEM((2, 4, ROWS, 256), BF),
            pltpu.VMEM((2, PAIRS, CELLS, 256), F32),
            pltpu.SemaphoreType.DMA((5,)),
        ],
        compiler_params=pltpu.CompilerParams(vmem_limit_bytes=CONV_VMEM_LIMIT),
        name="conv",
    )(planes, codes, hots, pair, jnp.asarray(fwd), jnp.asarray(rfwd), psf, jnp.asarray(rback), jnp.asarray(back))


def spread_kernel(meta_ref, back_ref, base_ref, out_hbm, done, sems):
    summed = back_ref[0:BLOCKS, :]
    for f in range(1, BANDS):
        summed = summed + back_ref[f * BLOCKS : (f + 1) * BLOCKS, :]
    meta = meta_ref[...]
    target, rank, right = meta[:, 0:1], meta[:, 1:2], meta[:, 2:3]
    lane64 = iota((SLOTS, 2 * BLOCKS), 1) & (BLOCKS - 1)
    hot = jnp.where(lane64 == target, 1.0, 0.0).astype(BF)
    picked = dot(hot, jnp.concatenate(split(summed), axis=0))
    lane = iota((SLOTS, 128), 1)
    picked = jnp.where((lane >> 4) == rank, picked, 0.0)
    plain = jnp.where(right == 1, picked, 0.0)
    sides = jnp.concatenate(split(plain) + split(picked - plain), axis=1)
    krow, nlane = iota((512, 128), 0), iota((512, 128), 1)
    have_j = (krow >> 2) & 3
    have_j = jnp.where(krow >= 256, 3 - have_j, have_j)
    match = have_j == ((nlane >> 4) & 3)
    stores = []
    for i in range(4):
        value = dot(sides, jnp.where(match & ((krow & 3) == i), 1.0, 0.0).astype(BF))
        for h in range(2):
            for m in range(4):
                at = i * 1024 + h * 512 + m * 128
                done[:, at : at + 128] = (base_ref[:, at : at + 128].astype(F32) + value).astype(BF)
            lanes = pl.ds(i * 1024 + h * 512, 512)
            stores.append(
                pltpu.make_async_copy(done.at[:, lanes], out_hbm.at[:, lanes], sems.at[2 * i + h])
            )
            stores[-1].start()
    for store in stores:
        store.wait()


def spread(meta, returned, base_grad):
    vmem_spec = pl.BlockSpec(memory_space=pltpu.VMEM)
    return pl.pallas_call(
        spread_kernel,
        out_shape=jax.ShapeDtypeStruct((SLOTS, 4096), BF),
        in_specs=[vmem_spec, vmem_spec, vmem_spec],
        out_specs=pl.BlockSpec(memory_space=pltpu.HBM),
        scratch_shapes=[pltpu.VMEM((SLOTS, 4096), BF), pltpu.SemaphoreType.DMA((8,))],
        compiler_params=pltpu.CompilerParams(vmem_limit_bytes=16 * 1024 * 1024),
        name="spread",
    )(meta, returned, base_grad)


def exchange(x, groups=None):
    return lax.all_to_all(
        x, ("fft", "tiles"), split_axis=0, concat_axis=0, axis_index_groups=groups, tiled=True
    )


def local(cotangent, base_grad, tile_place, tile_count, psf_spectrum):
    message, meta = pool(cotangent, tile_place, tile_count)
    groups = [[f * BLOCKS + t for f in range(c, BANDS, 2) for t in range(BLOCKS)] for c in range(2)]
    near = exchange(message.reshape(PAIRS * BLOCKS, 4, 128), groups).reshape(-1, 128)
    pair = lax.ppermute(near, "fft", [(f, f ^ 1) for f in range(BANDS)])
    planes, codes, hots = first(near)
    partial = conv(planes, codes, hots, pair, psf_spectrum)
    returned = exchange(partial)
    return spread(meta, returned, base_grad)


def solution(mesh):
    return jax.shard_map(
        local,
        mesh=mesh,
        in_specs=(
            P(("tiles", "fft"), None),
            P(("tiles", "fft"), None),
            P(("tiles", "fft")),
            P(("tiles", "fft")),
            P(None, None, "fft"),
        ),
        out_specs=P(("tiles", "fft"), None),
        check_vma=False,
    )
```
